32 devices in a mesh: slab: 4 (over y, core), angle: 8 (over z, x).
Axes of the slice: x: 2, y: 2, z: 4, core: 2. Of those that a mesh axis runs over, the one named last changes fastest.
Arguments:
- volume: float32 [1024, 128], P(('slab', 'angle')), may hold values from -6 to 6
- measured: float32 [512, 128], P('angle'), may hold values from 30 to 1000
- footprint: bfloat16 [6144, 128, 128], P(('slab', 'angle')), may hold values from 0.0099487305 to 1
- block_voxel: int32 [6144], P(('slab', 'angle')), may hold values from 0 to 255, as said below
- block_tile: int32 [6144], P(('slab', 'angle')), may hold values from 0 to 63
- block_rows: int32 [6144], P(('slab', 'angle')), may hold values from 0 to 128, as said below
Outputs:
- new_volume: float32 [1024, 128], P(('slab', 'angle'))
- weighted_residual: float32 [512, 128], P('angle')
The draws below stay inside these ranges and needn't reach their ends.
Inputs may be any that keep to these rules, and one draw needn't show every extreme that they name: `block_rows`: 0 marks an empty slot; the live slots of each device come first, each device has at least 48 live slots, some device has all 192 live, and every device has a live slot covering all 128 rows. On each device the slots form aligned groups of 48 in a row whose voxel blocks all lie in one share block_voxel // 32, different groups of a device in different shares; so at most 48 slots of a device name one share, and in each slab one share is named by 48 slots of every device.
All inputs are finite; a program needn't handle non-finite values.
Results may differ from the reference program's by a relative error of at most 0.00042.
Values may be sent and summed in bfloat16 or wider, within the bound.
A program may use at most 64 MiB of HBM per device.

```python
import math
import jax
import jax.numpy as jnp
from jax import lax

BLK = 128
VBD = 32
PTD = 64
NB = 192
CAP = 48
VB_SLAB = 256
VBLOCKS = 1024
TILES = 512
SLOTS = 6144
N_SLAB = 4
N_ANGLE = 8


def draw_block_rows(key, part):
    key = jax.random.fold_in(key, 7)
    key_rows, key_full, key_live, key_busy = jax.random.split(key, 4)
    device_count = SLOTS // NB
    slot_ids = jnp.arange(NB, dtype=jnp.int32)
    counts = jax.random.randint(key_rows, (device_count, NB), 1, BLK + 1)
    full_slot = jax.random.randint(key_full, (device_count,), 0, NB // 4)
    counts = jnp.where(slot_ids[None, :] == full_slot[:, None], BLK, counts)
    live_slots = jax.random.randint(key_live, (device_count,), NB // 4, NB + 1)
    busiest = jax.random.randint(key_busy, (), 0, device_count)
    live_slots = jnp.where(jnp.arange(device_count, dtype=jnp.int32) == busiest, NB, live_slots)
    counts = jnp.where(slot_ids[None, :] < live_slots[:, None], counts, 0)
    return counts.reshape(SLOTS).astype(jnp.int32)


def draw_block_voxel(key, part):
    key = jax.random.fold_in(key, 11)
    key_common, key_order, key_within = jax.random.split(key, 3)
    device_count = SLOTS // NB
    group_count = NB // CAP
    common = jax.random.randint(key_common, (), 0, N_ANGLE)
    order_keys = jax.random.split(key_order, device_count)
    shuffled = jax.vmap(lambda k: jax.random.permutation(k, N_ANGLE - 1))(order_keys).astype(jnp.int32) + 1
    offsets = jnp.concatenate([jnp.zeros((device_count, 1), jnp.int32), shuffled], 1)[:, :group_count]
    owners = (common + offsets) % N_ANGLE
    owner_slot = jnp.repeat(owners, CAP, axis=1)
    within = jax.random.randint(key_within, (device_count, NB), 0, VBD)
    return (owner_slot * VBD + within).reshape(SLOTS).astype(jnp.int32)


def with_ends(entries, stream_key, smallest, high):
    longest = entries.shape.index(max(entries.shape))
    spots = []
    for shift in (0, 1):
        where = [jax.random.randint(jax.random.fold_in(stream_key, axis), (), 0, length) for axis, length in enumerate(entries.shape)]
        where[longest] = (where[longest] + shift) % entries.shape[longest]
        spots.append(tuple(where))
    return entries.at[spots[0]].set(smallest).at[spots[1]].set(high)


def block_levels(rng, dims, cuts, smallest, largest):
    loudness, own = 1.0, jax.random.fold_in(rng, 6)
    for dim, blocks in cuts:
        steps = jnp.exp(jax.random.uniform(jax.random.fold_in(own, dim), (blocks,), jnp.float32, smallest / len(cuts), largest / len(cuts)))
        loudness = loudness * jnp.repeat(steps, dims[dim] // blocks).reshape([-1 if axis == dim else 1 for axis in range(len(dims))])
    return loudness


def bell_draw(own_key, dims, spread, limit, pieces=(), kind=jnp.bfloat16):
    entries = spread * jax.random.normal(own_key, dims, jnp.float32)
    if pieces:
        entries = entries * block_levels(own_key, dims, pieces, -0.22, 0.18)
    return jnp.clip(entries, -limit, limit).astype(kind)


def setup_inputs(seed: int = 0) -> dict:
    arg_keys = jax.random.split(jax.random.key(seed), 7)
    volume = bell_draw(arg_keys[0], (VBLOCKS, BLK), 1.0, 6.0, ((0, 32),), jnp.float32)
    measured = jnp.clip(jnp.exp(math.log(1000.0) - 3.506558 * jax.random.uniform(arg_keys[1], (TILES, BLK), jnp.float32) ** block_levels(arg_keys[1], (TILES, BLK), ((0, 8),), -0.2, 0.2)), 30.0, 1000.0)
    footprint = jnp.clip(jnp.exp(math.log(1.0) - 4.61031033 * jax.random.uniform(arg_keys[2], (SLOTS, BLK, BLK), jnp.float32) ** block_levels(arg_keys[2], (SLOTS, BLK, BLK), ((0, 32),), -0.2, 0.2)), 0.0099487305, 1.0).astype(jnp.bfloat16)
    block_voxel = draw_block_voxel(jax.random.fold_in(arg_keys[6], 71), 0)
    block_tile = with_ends(jax.random.randint(arg_keys[4], (SLOTS,), 0, PTD), jax.random.fold_in(arg_keys[4], 1), 0, PTD - 1).astype(jnp.int32)
    block_rows = draw_block_rows(jax.random.fold_in(arg_keys[6], 71), 0)
    return {"volume": volume, "measured": measured, "footprint": footprint, "block_voxel": block_voxel, "block_tile": block_tile, "block_rows": block_rows}


def reference(volume, measured, footprint, block_voxel, block_tile, block_rows):
    device_count = N_SLAB * N_ANGLE
    owner = jnp.arange(SLOTS, dtype=jnp.int32) // NB
    glob_voxel = ((owner // N_ANGLE) * VB_SLAB + block_voxel).astype(jnp.int32)
    glob_tile = ((owner % N_ANGLE) * PTD + block_tile).astype(jnp.int32)
    row_live = (jnp.arange(BLK, dtype=jnp.int32)[None, :] < block_rows[:, None]).astype(jnp.float32)
    coarse = lax.optimization_barrier(volume.astype(jnp.bfloat16)).astype(jnp.float32)
    mats_all = footprint.reshape(device_count, NB, BLK, BLK)
    voxels_all = glob_voxel.reshape(device_count, NB)
    tiles_all = glob_tile.reshape(device_count, NB)
    live_all = row_live.reshape(device_count, NB, BLK)

    def forward_step(total, items):
        mats, voxels, tiles, live_rows = items
        picked = coarse[voxels]
        stacked = jnp.stack([picked, jnp.ones_like(picked)], 1)
        contrib = jnp.einsum('bpv,bkv->bkp', mats.astype(jnp.float32), stacked, precision=lax.Precision.HIGHEST)
        contrib = contrib * live_rows[:, None, :]
        return total.at[tiles].add(contrib), None

    totals, _ = lax.scan(forward_step, jnp.zeros((TILES, 2, BLK), jnp.float32), (mats_all, voxels_all, tiles_all, live_all))
    weighted = (measured - totals[:, 0]) / jnp.maximum(totals[:, 1], 1.0)
    coarse_res = lax.optimization_barrier(weighted.astype(jnp.bfloat16)).astype(jnp.float32)

    def backward_step(total, items):
        mats, voxels, tiles, live_rows = items
        picked = coarse_res[tiles] * live_rows
        stacked = jnp.stack([picked, live_rows], 1)
        contrib = jnp.einsum('bpv,bkp->bkv', mats.astype(jnp.float32), stacked, precision=lax.Precision.HIGHEST)
        return total.at[voxels].add(contrib), None

    backs, _ = lax.scan(backward_step, jnp.zeros((VBLOCKS, 2, BLK), jnp.float32), (mats_all, voxels_all, tiles_all, live_all))
    correction = backs[:, 0] / jnp.maximum(backs[:, 1], 1.0)
    return volume + correction, weighted
```

```python
import functools

import jax
import jax.numpy as jnp
from jax import lax
from jax.experimental import pallas as pl
from jax.experimental.pallas import tpu as pltpu
from jax.sharding import PartitionSpec as P

MESH = pl.DeviceIdType.MESH
F32 = jnp.float32
BF16 = jnp.bfloat16
FWD = 16
BWD = 12
PIECES = 4


def dot(a, b):
    return jnp.dot(a, b, preferred_element_type=F32)


def dot_nt(a, b):
    return lax.dot_general(a, b, (((1,), (1,)), ((), ())), preferred_element_type=F32)


def three_terms(x):
    hi = x.astype(BF16)
    rest = x - hi.astype(F32)
    mid = rest.astype(BF16)
    lo = (rest - mid.astype(F32)).astype(BF16)
    return hi, mid, lo


def kernel(
    n_slab, n_angle, cap,
    vol_hbm, meas_hbm, foot_hbm, voxel_hbm, tile_hbm, rows_hbm,
    new_hbm, res_hbm,
    w, vol, meas, voxel_v, tile_v, rows_v, voxel_s,
    slab_vals, picked, live, fwd, onehot_t, row_parts, proj_parts,
    col_out, col_in, back_out, back_in, res_buf, new_buf,
    piece_sem, local_sem, out_sem,
    vals_send, vals_recv, row_send, row_recv, proj_send, proj_recv,
    col_send, col_recv, back_send, back_recv,
):
    slots, width, _ = w.shape
    kept = vol.shape[0]
    tiles = meas.shape[0]
    groups = slots // cap
    piece = slots // PIECES
    my_slab = lax.axis_index("slab")
    my_angle = lax.axis_index("angle")

    def angle_peer(d):
        return lax.rem(my_angle + d, n_angle)

    def slab_peer(d):
        return lax.rem(my_slab + d, n_slab)

    vol_copy = pltpu.make_async_copy(vol_hbm, vol, local_sem.at[0])
    vol_copy.start()
    index_copies = [
        pltpu.make_async_copy(voxel_hbm, voxel_v, local_sem.at[1]),
        pltpu.make_async_copy(tile_hbm, tile_v, local_sem.at[2]),
        pltpu.make_async_copy(rows_hbm, rows_v, local_sem.at[3]),
        pltpu.make_async_copy(voxel_hbm, voxel_s, local_sem.at[4]),
    ]
    for c in index_copies:
        c.start()
    piece_copies = []
    for i in range(PIECES):
        span = pl.ds(i * piece, piece)
        c = pltpu.make_async_copy(foot_hbm.at[span], w.at[span], piece_sem.at[i])
        c.start()
        piece_copies.append(c)
    meas_copy = pltpu.make_async_copy(meas_hbm, meas, local_sem.at[5])
    meas_copy.start()

    barrier = pltpu.get_barrier_semaphore()
    for d in range(1, n_angle):
        pl.semaphore_signal(barrier, inc=1, device_id={"angle": angle_peer(d)}, device_id_type=MESH)
    for d in range(1, n_slab):
        pl.semaphore_signal(barrier, inc=1, device_id={"slab": slab_peer(d)}, device_id_type=MESH)
    vol_copy.wait()
    slab_vals[my_angle] = vol[...].astype(BF16)
    pl.semaphore_wait(barrier, n_angle + n_slab - 2)

    vals_copies = []
    for d in range(1, n_angle):
        c = pltpu.make_async_remote_copy(
            src_ref=slab_vals.at[my_angle], dst_ref=slab_vals.at[my_angle],
            send_sem=vals_send.at[d - 1], recv_sem=vals_recv.at[d - 1],
            device_id={"angle": angle_peer(d)}, device_id_type=MESH,
        )
        c.start()
        vals_copies.append(c)

    def slab_exchange(buf, send, recv):
        copies = []
        for d in range(1, n_slab):
            c = pltpu.make_async_remote_copy(
                src_ref=buf.at[my_slab], dst_ref=buf.at[my_slab],
                send_sem=send.at[d - 1], recv_sem=recv.at[d - 1],
                device_id={"slab": slab_peer(d)}, device_id_type=MESH,
            )
            c.start()
            copies.append(c)
        return copies

    def angle_exchange(out, into, send, recv):
        copies = []
        for d in range(1, n_angle):
            c = pltpu.make_async_remote_copy(
                src_ref=out.at[angle_peer(d)], dst_ref=into.at[my_angle],
                send_sem=send.at[d - 1], recv_sem=recv.at[d - 1],
                device_id={"angle": angle_peer(d)}, device_id_type=MESH,
            )
            c.start()
            copies.append(c)
        return copies

    for c in index_copies:
        c.wait()

    def down(ref):
        return jnp.broadcast_to(ref[...].astype(F32), (width, slots)).T

    voxel_col = down(voxel_v)
    tile_col = down(tile_v)
    lane = lax.broadcasted_iota(jnp.int32, (slots, width), 1).astype(F32)
    live[...] = jnp.where(lane < down(rows_v), 1.0, 0.0)
    tile_rows = lax.broadcasted_iota(jnp.int32, (tiles, slots), 0)
    onehot_t[...] = jnp.where(tile_rows == tile_v[...], 1.0, 0.0).astype(BF16)

    def scatter_tiles(values):
        terms = jnp.concatenate(three_terms(values), axis=1)
        out = dot(onehot_t[...], terms)
        return (out[:, 2 * width :] + out[:, width : 2 * width]) + out[:, :width]

    row_id = lax.broadcasted_iota(jnp.int32, (FWD, width), 0)

    def forward_step(k0, left):
        mats = w[pl.ds(k0, FWD)].reshape(FWD * width, width)
        prod = dot_nt(left, mats)
        out = prod[:, :width]
        for i in range(1, FWD):
            out = jnp.where(row_id == i, prod[:, i * width : (i + 1) * width], out)
        fwd[pl.ds(k0, FWD), :] = out

    ones = jnp.ones((FWD, width), BF16)
    for i in range(PIECES):
        piece_copies[i].wait()
        for k0 in range(i * piece, (i + 1) * piece, FWD):
            forward_step(k0, ones)
    row_parts[my_slab] = scatter_tiles(fwd[...] * live[...])
    row_copies = slab_exchange(row_parts, row_send, row_recv)

    for c in vals_copies:
        c.wait_recv()
    all_vals = slab_vals[...].reshape(n_angle * kept, width)
    sums = jnp.zeros((slots, width), F32)
    for j0 in range(0, n_angle * kept, width):
        sel = jnp.where(voxel_col == lane + float(j0), 1.0, 0.0).astype(BF16)
        sums = sums + dot(sel, all_vals[j0 : j0 + width])
    picked[...] = sums.astype(BF16)
    for k0 in range(0, slots, FWD):
        forward_step(k0, picked[pl.ds(k0, FWD), :])
    proj_parts[my_slab] = scatter_tiles(fwd[...] * live[...])
    proj_copies = slab_exchange(proj_parts, proj_send, proj_recv)

    block_id = lax.broadcasted_iota(jnp.int32, (kept, width), 0)

    def backward(rows_ref, out_ref):
        totals = []
        shares = []
        for g in range(groups):
            share = lax.div(voxel_s[0, g * cap], kept)
            ids = block_id + share * kept
            total = jnp.zeros((kept, width), F32)
            for k0 in range(g * cap, (g + 1) * cap, BWD):
                cols = []
                for k in range(k0, k0 + BWD):
                    row = jnp.broadcast_to(rows_ref[k : k + 1, :], (kept, width))
                    cols.append(jnp.where(ids == voxel_s[0, k], row, 0.0).astype(BF16))
                mats = w[pl.ds(k0, BWD)].reshape(BWD * width, width)
                total = total + dot(jnp.concatenate(cols, axis=1), mats)
            totals.append(total)
            shares.append(jnp.full((kept, width), share, jnp.int32))
        for s in range(n_angle):
            out = jnp.where(shares[0] == s, totals[0], 0.0)
            for g in range(1, groups):
                out = jnp.where(shares[g] == s, totals[g], out)
            out_ref[s] = out

    backward(live, col_out)
    col_copies = angle_exchange(col_out, col_in, col_send, col_recv)

    meas_copy.wait()
    for c in row_copies:
        c.wait()
    row_sum = row_parts[0]
    for s in range(1, n_slab):
        row_sum = row_sum + row_parts[s]
    row_sum = jnp.maximum(row_sum, 1.0)
    for c in proj_copies:
        c.wait()
    proj = proj_parts[0]
    for s in range(1, n_slab):
        proj = proj + proj_parts[s]
    weighted = (meas[...] - proj) / row_sum
    res_buf[...] = weighted
    res_copy = pltpu.make_async_copy(res_buf, res_hbm, out_sem.at[0])
    res_copy.start()
    sel = jnp.where(tile_col == lane, 1.0, 0.0)[:, :tiles].astype(BF16)
    fwd[...] = dot(sel, weighted.astype(BF16)) * live[...]
    backward(fwd, back_out)
    back_copies = angle_exchange(back_out, back_in, back_send, back_recv)

    back_in[my_angle] = back_out[my_angle]
    col_in[my_angle] = col_out[my_angle]
    for c in col_copies:
        c.wait()
    col_sum = col_in[0]
    for s in range(1, n_angle):
        col_sum = col_sum + col_in[s]
    col_sum = jnp.maximum(col_sum, 1.0)
    for c in back_copies:
        c.wait_recv()
    back = back_in[0]
    for s in range(1, n_angle):
        back = back + back_in[s]
    new_buf[...] = vol[...] + back / col_sum
    new_copy = pltpu.make_async_copy(new_buf, new_hbm, out_sem.at[1])
    new_copy.start()
    for c in vals_copies:
        c.wait_send()
    for c in back_copies:
        c.wait_send()
    res_copy.wait()
    new_copy.wait()


def on_device(volume, measured, footprint, block_voxel, block_tile, block_rows):
    n_slab = lax.axis_size("slab")
    n_angle = lax.axis_size("angle")
    kept, width = volume.shape
    tiles = measured.shape[0]
    slots = footprint.shape[0]
    cap = 2 * slots // n_angle
    dma = pltpu.SemaphoreType.DMA
    any_space = pl.BlockSpec(memory_space=pl.ANY)
    index = pltpu.VMEM((1, slots), jnp.int32)
    per_share = pltpu.VMEM((n_angle, kept, width), F32)
    per_slab = pltpu.VMEM((n_slab, tiles, width), F32)
    by_slot = pltpu.VMEM((slots, width), F32)
    return pl.pallas_call(
        functools.partial(kernel, n_slab, n_angle, cap),
        out_shape=(
            jax.ShapeDtypeStruct(volume.shape, F32),
            jax.ShapeDtypeStruct(measured.shape, F32),
        ),
        in_specs=[any_space] * 6,
        out_specs=(any_space, any_space),
        scratch_shapes=[
            pltpu.VMEM(footprint.shape, BF16),
            pltpu.VMEM(volume.shape, F32),
            pltpu.VMEM(measured.shape, F32),
            index, index, index,
            pltpu.SMEM((1, slots), jnp.int32),
            pltpu.VMEM((n_angle, kept, width), BF16),
            pltpu.VMEM((slots, width), BF16),
            by_slot, by_slot,
            pltpu.VMEM((tiles, slots), BF16),
            per_slab, per_slab,
            per_share, per_share, per_share, per_share,
            pltpu.VMEM(measured.shape, F32),
            pltpu.VMEM(volume.shape, F32),
            dma((PIECES,)), dma((6,)), dma((2,)),
            dma((n_angle - 1,)), dma((n_angle - 1,)),
            dma((n_slab - 1,)), dma((n_slab - 1,)),
            dma((n_slab - 1,)), dma((n_slab - 1,)),
            dma((n_angle - 1,)), dma((n_angle - 1,)),
            dma((n_angle - 1,)), dma((n_angle - 1,)),
        ],
        compiler_params=pltpu.CompilerParams(
            collective_id=0, has_side_effects=True, vmem_limit_bytes=56 * 1024 * 1024
        ),
        cost_estimate=pl.CostEstimate(
            flops=8 * slots * width * width, bytes_accessed=2 * slots * width * width, transcendentals=0
        ),
    )(
        volume, measured, footprint,
        block_voxel.reshape(1, slots), block_tile.reshape(1, slots), block_rows.reshape(1, slots),
    )


def solution(mesh):
    in_specs = (
        P(("slab", "angle"), None),
        P("angle", None),
        P(("slab", "angle"), None, None),
        P(("slab", "angle")),
        P(("slab", "angle")),
        P(("slab", "angle")),
    )
    out_specs = (P(("slab", "angle"), None), P("angle", None))
    return jax.shard_map(
        on_device, mesh=mesh, in_specs=in_specs, out_specs=out_specs, check_vma=False
    )
```

```python
import functools

import jax
import jax.numpy as jnp
from jax import lax
from jax.experimental import pallas as pl
from jax.experimental.pallas import tpu as pltpu
from jax.sharding import PartitionSpec as P

MESH = pl.DeviceIdType.MESH
F32 = jnp.float32
BF16 = jnp.bfloat16
FWD = 16
BWD = 12
PIECES = 4


def dot(a, b):
    return jnp.dot(a, b, preferred_element_type=F32)


def dot_nt(a, b):
    return lax.dot_general(a, b, (((1,), (1,)), ((), ())), preferred_element_type=F32)


def three_terms(x):
    hi = x.astype(BF16)
    rest = x - hi.astype(F32)
    mid = rest.astype(BF16)
    lo = (rest - mid.astype(F32)).astype(BF16)
    return hi, mid, lo


def kernel(
    n_slab, n_angle, cap,
    vol_hbm, meas_hbm, foot_hbm, voxel_hbm, tile_hbm, rows_hbm,
    new_hbm, res_hbm,
    w, vol, meas, voxel_v, tile_v, rows_v, voxel_s,
    slab_vals, picked, live, fwd, onehot_t, row_parts, proj_parts,
    col_out, col_in, back_out, back_in, res_buf, new_buf, left_live,
    piece_sem, local_sem, out_sem,
    vals_send, vals_recv, row_send, row_recv, proj_send, proj_recv,
    col_send, col_recv, back_send, back_recv,
):
    slots, width, _ = w.shape
    kept = vol.shape[0]
    tiles = meas.shape[0]
    groups = slots // cap
    piece = slots // PIECES
    my_slab = lax.axis_index("slab")
    my_angle = lax.axis_index("angle")

    def angle_peer(d):
        return lax.rem(my_angle + d, n_angle)

    def slab_peer(d):
        return lax.rem(my_slab + d, n_slab)

    vol_copy = pltpu.make_async_copy(vol_hbm, vol, local_sem.at[0])
    vol_copy.start()
    index_copies = [
        pltpu.make_async_copy(voxel_hbm, voxel_v, local_sem.at[1]),
        pltpu.make_async_copy(tile_hbm, tile_v, local_sem.at[2]),
        pltpu.make_async_copy(rows_hbm, rows_v, local_sem.at[3]),
        pltpu.make_async_copy(voxel_hbm, voxel_s, local_sem.at[4]),
    ]
    for c in index_copies:
        c.start()
    piece_copies = []
    for i in range(PIECES):
        span = pl.ds(i * piece, piece)
        c = pltpu.make_async_copy(foot_hbm.at[span], w.at[span], piece_sem.at[i])
        c.start()
        piece_copies.append(c)
    meas_copy = pltpu.make_async_copy(meas_hbm, meas, local_sem.at[5])
    meas_copy.start()

    barrier = pltpu.get_barrier_semaphore()
    for d in range(1, n_angle):
        pl.semaphore_signal(barrier, inc=1, device_id={"angle": angle_peer(d)}, device_id_type=MESH)
    for d in range(1, n_slab):
        pl.semaphore_signal(barrier, inc=1, device_id={"slab": slab_peer(d)}, device_id_type=MESH)
    vol_copy.wait()
    slab_vals[my_angle] = vol[...].astype(BF16)
    pl.semaphore_wait(barrier, n_angle + n_slab - 2)

    vals_copies = []
    for d in range(1, n_angle):
        c = pltpu.make_async_remote_copy(
            src_ref=slab_vals.at[my_angle], dst_ref=slab_vals.at[my_angle],
            send_sem=vals_send.at[d - 1], recv_sem=vals_recv.at[d - 1],
            device_id={"angle": angle_peer(d)}, device_id_type=MESH,
        )
        c.start()
        vals_copies.append(c)

    def slab_exchange(buf, send, recv):
        copies = []
        for d in range(1, n_slab):
            c = pltpu.make_async_remote_copy(
                src_ref=buf.at[my_slab], dst_ref=buf.at[my_slab],
                send_sem=send.at[d - 1], recv_sem=recv.at[d - 1],
                device_id={"slab": slab_peer(d)}, device_id_type=MESH,
            )
            c.start()
            copies.append(c)
        return copies

    def angle_exchange(out, into, send, recv):
        copies = []
        for d in range(1, n_angle):
            c = pltpu.make_async_remote_copy(
                src_ref=out.at[angle_peer(d)], dst_ref=into.at[my_angle],
                send_sem=send.at[d - 1], recv_sem=recv.at[d - 1],
                device_id={"angle": angle_peer(d)}, device_id_type=MESH,
            )
            c.start()
            copies.append(c)
        return copies

    for c in index_copies:
        c.wait()

    def down(ref):
        return jnp.broadcast_to(ref[...].astype(F32), (width, slots)).T

    voxel_col = down(voxel_v)
    tile_col = down(tile_v)
    lane = lax.broadcasted_iota(jnp.int32, (slots, width), 1).astype(F32)
    live[...] = jnp.where(lane < down(rows_v), 1.0, 0.0)
    tile_rows = lax.broadcasted_iota(jnp.int32, (tiles, slots), 0)
    onehot_t[...] = jnp.where(tile_rows == tile_v[...], 1.0, 0.0).astype(BF16)

    def scatter_tiles(values):
        terms = jnp.concatenate(three_terms(values), axis=1)
        out = dot(onehot_t[...], terms)
        return (out[:, 2 * width :] + out[:, width : 2 * width]) + out[:, :width]

    row_id = lax.broadcasted_iota(jnp.int32, (FWD, width), 0)

    def forward_step(k0, left):
        mats = w[pl.ds(k0, FWD)].reshape(FWD * width, width)
        prod = dot_nt(left, mats)
        out = prod[:, :width]
        for i in range(1, FWD):
            out = jnp.where(row_id == i, prod[:, i * width : (i + 1) * width], out)
        fwd[pl.ds(k0, FWD), :] = out

    ones = jnp.ones((FWD, width), BF16)
    for i in range(PIECES):
        piece_copies[i].wait()
        for k0 in range(i * piece, (i + 1) * piece, FWD):
            forward_step(k0, ones)
    row_parts[my_slab] = scatter_tiles(fwd[...] * live[...])
    row_copies = slab_exchange(row_parts, row_send, row_recv)

    for c in vals_copies:
        c.wait_recv()
    all_vals = slab_vals[...].reshape(n_angle * kept, width)
    sums = jnp.zeros((slots, width), F32)
    for j0 in range(0, n_angle * kept, width):
        sel = jnp.where(voxel_col == lane + float(j0), 1.0, 0.0).astype(BF16)
        sums = sums + dot(sel, all_vals[j0 : j0 + width])
    picked[...] = sums.astype(BF16)
    for k0 in range(0, slots, FWD):
        forward_step(k0, picked[pl.ds(k0, FWD), :])
    proj_parts[my_slab] = scatter_tiles(fwd[...] * live[...])
    proj_copies = slab_exchange(proj_parts, proj_send, proj_recv)

    block_id = lax.broadcasted_iota(jnp.int32, (kept, width), 0)

    def live_left(k, ids):
        row = jnp.broadcast_to(live[k : k + 1, :], (kept, width))
        left = jnp.where(ids == voxel_s[0, k], row, 0.0).astype(BF16)
        left_live[k] = left
        return left

    def residual_left(k, ids):
        row = jnp.broadcast_to(fwd[k : k + 1, :], (kept, width))
        return left_live[k] * row.astype(BF16)

    def backward(left_of, out_ref):
        totals = []
        shares = []
        for g in range(groups):
            share = lax.div(voxel_s[0, g * cap], kept)
            ids = block_id + share * kept
            total = jnp.zeros((kept, width), F32)
            for k0 in range(g * cap, (g + 1) * cap, BWD):
                cols = [left_of(k, ids) for k in range(k0, k0 + BWD)]
                mats = w[pl.ds(k0, BWD)].reshape(BWD * width, width)
                total = total + dot(jnp.concatenate(cols, axis=1), mats)
            totals.append(total)
            shares.append(jnp.full((kept, width), share, jnp.int32))
        for s in range(n_angle):
            out = jnp.where(shares[0] == s, totals[0], 0.0)
            for g in range(1, groups):
                out = jnp.where(shares[g] == s, totals[g], out)
            out_ref[s] = out

    backward(live_left, col_out)
    col_copies = angle_exchange(col_out, col_in, col_send, col_recv)

    meas_copy.wait()
    for c in row_copies:
        c.wait()
    row_sum = row_parts[0]
    for s in range(1, n_slab):
        row_sum = row_sum + row_parts[s]
    row_sum = jnp.maximum(row_sum, 1.0)
    for c in proj_copies:
        c.wait()
    proj = proj_parts[0]
    for s in range(1, n_slab):
        proj = proj + proj_parts[s]
    weighted = (meas[...] - proj) / row_sum
    res_buf[...] = weighted
    res_copy = pltpu.make_async_copy(res_buf, res_hbm, out_sem.at[0])
    res_copy.start()
    sel = jnp.where(tile_col == lane, 1.0, 0.0)[:, :tiles].astype(BF16)
    fwd[...] = dot(sel, weighted.astype(BF16))
    backward(residual_left, back_out)
    back_copies = angle_exchange(back_out, back_in, back_send, back_recv)

    back_in[my_angle] = back_out[my_angle]
    col_in[my_angle] = col_out[my_angle]
    for c in col_copies:
        c.wait()
    col_sum = col_in[0]
    for s in range(1, n_angle):
        col_sum = col_sum + col_in[s]
    col_sum = jnp.maximum(col_sum, 1.0)
    for c in back_copies:
        c.wait_recv()
    back = back_in[0]
    for s in range(1, n_angle):
        back = back + back_in[s]
    new_buf[...] = vol[...] + back / col_sum
    new_copy = pltpu.make_async_copy(new_buf, new_hbm, out_sem.at[1])
    new_copy.start()
    for c in vals_copies:
        c.wait_send()
    for c in back_copies:
        c.wait_send()
    res_copy.wait()
    new_copy.wait()


def hand_over(new_in, res_in, new_hbm, res_hbm, sem):
    copies = [
        pltpu.make_async_copy(new_in, new_hbm, sem.at[0]),
        pltpu.make_async_copy(res_in, res_hbm, sem.at[1]),
    ]
    for c in copies:
        c.start()
    for c in copies:
        c.wait()


def on_device(volume, measured, footprint, block_voxel, block_tile, block_rows):
    n_slab = lax.axis_size("slab")
    n_angle = lax.axis_size("angle")
    kept, width = volume.shape
    tiles = measured.shape[0]
    slots = footprint.shape[0]
    cap = 2 * slots // n_angle
    any_space = pl.BlockSpec(memory_space=pl.ANY)
    dma = pltpu.SemaphoreType.DMA
    index = pltpu.VMEM((1, slots), jnp.int32)
    per_share = pltpu.VMEM((n_angle, kept, width), F32)
    per_slab = pltpu.VMEM((n_slab, tiles, width), F32)
    by_slot = pltpu.VMEM((slots, width), F32)
    new, res = pl.pallas_call(
        functools.partial(kernel, n_slab, n_angle, cap),
        out_shape=(
            jax.ShapeDtypeStruct(volume.shape, F32),
            jax.ShapeDtypeStruct(measured.shape, F32),
        ),
        in_specs=[any_space] * 6,
        out_specs=(any_space, any_space),
        scratch_shapes=[
            pltpu.VMEM(footprint.shape, BF16),
            pltpu.VMEM(volume.shape, F32),
            pltpu.VMEM(measured.shape, F32),
            index, index, index,
            pltpu.SMEM((1, slots), jnp.int32),
            pltpu.VMEM((n_angle, kept, width), BF16),
            pltpu.VMEM((slots, width), BF16),
            by_slot, by_slot,
            pltpu.VMEM((tiles, slots), BF16),
            per_slab, per_slab,
            per_share, per_share, per_share, per_share,
            pltpu.VMEM(measured.shape, F32),
            pltpu.VMEM(volume.shape, F32),
            pltpu.VMEM((slots, kept, width), BF16),
            dma((PIECES,)), dma((6,)), dma((2,)),
            dma((n_angle - 1,)), dma((n_angle - 1,)),
            dma((n_slab - 1,)), dma((n_slab - 1,)),
            dma((n_slab - 1,)), dma((n_slab - 1,)),
            dma((n_angle - 1,)), dma((n_angle - 1,)),
            dma((n_angle - 1,)), dma((n_angle - 1,)),
        ],
        compiler_params=pltpu.CompilerParams(
            collective_id=0, has_side_effects=True, vmem_limit_bytes=56 * 1024 * 1024
        ),
        cost_estimate=pl.CostEstimate(
            flops=8 * slots * width * width, bytes_accessed=2 * slots * width * width, transcendentals=0
        ),
    )(
        volume, measured, footprint,
        block_voxel.reshape(1, slots), block_tile.reshape(1, slots), block_rows.reshape(1, slots),
    )
    return pl.pallas_call(
        hand_over,
        out_shape=(
            jax.ShapeDtypeStruct(volume.shape, F32),
            jax.ShapeDtypeStruct(measured.shape, F32),
        ),
        in_specs=[any_space] * 2,
        out_specs=(any_space, any_space),
        scratch_shapes=[dma((2,))],
        compiler_params=pltpu.CompilerParams(vmem_limit_bytes=56 * 1024 * 1024),
    )(new, res)


def solution(mesh):
    in_specs = (
        P(("slab", "angle"), None),
        P("angle", None),
        P(("slab", "angle"), None, None),
        P(("slab", "angle")),
        P(("slab", "angle")),
        P(("slab", "angle")),
    )
    out_specs = (P(("slab", "angle"), None), P("angle", None))
    return jax.shard_map(
        on_device, mesh=mesh, in_specs=in_specs, out_specs=out_specs, check_vma=False
    )
```

```python
import functools

import jax
import jax.numpy as jnp
from jax import lax
from jax.experimental import pallas as pl
from jax.experimental.pallas import tpu as pltpu
from jax.sharding import PartitionSpec as P

MESH = pl.DeviceIdType.MESH
F32 = jnp.float32
BF16 = jnp.bfloat16
FWD = 16
BWD = 12
PIECES = 4


def dot(a, b):
    return jnp.dot(a, b, preferred_element_type=F32)


def three_terms(x):
    hi = x.astype(BF16)
    rest = x - hi.astype(F32)
    mid = rest.astype(BF16)
    lo = (rest - mid.astype(F32)).astype(BF16)
    return hi, mid, lo


def kernel(
    n_slab, n_angle, cap,
    vol_hbm, meas_hbm, foot_hbm, voxel_hbm, tile_hbm, rows_hbm,
    new_hbm, res_hbm,
    w, w_turned, vol, meas, voxel_v, tile_v, rows_v, voxel_s,
    slab_vals, picked, live, fwd, onehot_t, row_parts, proj_parts,
    col_out, col_in, back_out, back_in, res_buf, new_buf, left_live,
    piece_sem, local_sem, out_sem,
    vals_send, vals_recv, row_send, row_recv, proj_send, proj_recv,
    col_send, col_recv, back_send, back_recv,
):
    slots, width, _ = w.shape
    kept = vol.shape[0]
    tiles = meas.shape[0]
    groups = slots // cap
    piece = slots // PIECES
    my_slab = lax.axis_index("slab")
    my_angle = lax.axis_index("angle")

    def angle_peer(d):
        return lax.rem(my_angle + d, n_angle)

    def slab_peer(d):
        return lax.rem(my_slab + d, n_slab)

    vol_copy = pltpu.make_async_copy(vol_hbm, vol, local_sem.at[0])
    vol_copy.start()
    index_copies = [
        pltpu.make_async_copy(voxel_hbm, voxel_v, local_sem.at[1]),
        pltpu.make_async_copy(tile_hbm, tile_v, local_sem.at[2]),
        pltpu.make_async_copy(rows_hbm, rows_v, local_sem.at[3]),
        pltpu.make_async_copy(voxel_hbm, voxel_s, local_sem.at[4]),
    ]
    for c in index_copies:
        c.start()
    piece_copies = []
    for i in range(PIECES):
        span = pl.ds(i * piece, piece)
        c = pltpu.make_async_copy(foot_hbm.at[span], w.at[span], piece_sem.at[i])
        c.start()
        piece_copies.append(c)
    meas_copy = pltpu.make_async_copy(meas_hbm, meas, local_sem.at[5])
    meas_copy.start()

    barrier = pltpu.get_barrier_semaphore()
    for d in range(1, n_angle):
        pl.semaphore_signal(barrier, inc=1, device_id={"angle": angle_peer(d)}, device_id_type=MESH)
    for d in range(1, n_slab):
        pl.semaphore_signal(barrier, inc=1, device_id={"slab": slab_peer(d)}, device_id_type=MESH)
    vol_copy.wait()
    slab_vals[my_angle] = vol[...].astype(BF16)
    pl.semaphore_wait(barrier, n_angle + n_slab - 2)

    vals_copies = []
    for d in range(1, n_angle):
        c = pltpu.make_async_remote_copy(
            src_ref=slab_vals.at[my_angle], dst_ref=slab_vals.at[my_angle],
            send_sem=vals_send.at[d - 1], recv_sem=vals_recv.at[d - 1],
            device_id={"angle": angle_peer(d)}, device_id_type=MESH,
        )
        c.start()
        vals_copies.append(c)

    def slab_exchange(buf, send, recv):
        copies = []
        for d in range(1, n_slab):
            c = pltpu.make_async_remote_copy(
                src_ref=buf.at[my_slab], dst_ref=buf.at[my_slab],
                send_sem=send.at[d - 1], recv_sem=recv.at[d - 1],
                device_id={"slab": slab_peer(d)}, device_id_type=MESH,
            )
            c.start()
            copies.append(c)
        return copies

    def angle_exchange(out, into, send, recv):
        copies = []
        for d in range(1, n_angle):
            c = pltpu.make_async_remote_copy(
                src_ref=out.at[angle_peer(d)], dst_ref=into.at[my_angle],
                send_sem=send.at[d - 1], recv_sem=recv.at[d - 1],
                device_id={"angle": angle_peer(d)}, device_id_type=MESH,
            )
            c.start()
            copies.append(c)
        return copies

    for c in index_copies:
        c.wait()

    def down(ref):
        return jnp.broadcast_to(ref[...].astype(F32), (width, slots)).T

    voxel_col = down(voxel_v)
    tile_col = down(tile_v)
    lane = lax.broadcasted_iota(jnp.int32, (slots, width), 1).astype(F32)
    live[...] = jnp.where(lane < down(rows_v), 1.0, 0.0)
    tile_rows = lax.broadcasted_iota(jnp.int32, (tiles, slots), 0)
    onehot_t[...] = jnp.where(tile_rows == tile_v[...], 1.0, 0.0).astype(BF16)

    def scatter_tiles(values):
        terms = jnp.concatenate(three_terms(values), axis=1)
        out = dot(onehot_t[...], terms)
        return (out[:, 2 * width :] + out[:, width : 2 * width]) + out[:, :width]

    row_id = lax.broadcasted_iota(jnp.int32, (FWD, width), 0)
    own_row = [jnp.where(row_id == i, 1.0, 0.0).astype(BF16) for i in range(FWD)]

    def forward_step(k0, left):
        mats = w_turned[pl.ds(k0, FWD)].reshape(FWD * width, width)
        fwd[pl.ds(k0, FWD), :] = dot(jnp.concatenate(left, axis=1), mats)

    for i in range(PIECES):
        piece_copies[i].wait()
        for k0 in range(i * piece, (i + 1) * piece, FWD):
            for k in range(k0, k0 + FWD):
                w_turned[k] = w[k].T
            forward_step(k0, own_row)
    row_parts[my_slab] = scatter_tiles(fwd[...] * live[...])
    row_copies = slab_exchange(row_parts, row_send, row_recv)

    for c in vals_copies:
        c.wait_recv()
    all_vals = slab_vals[...].reshape(n_angle * kept, width)
    sums = jnp.zeros((slots, width), F32)
    for j0 in range(0, n_angle * kept, width):
        sel = jnp.where(voxel_col == lane + float(j0), 1.0, 0.0).astype(BF16)
        sums = sums + dot(sel, all_vals[j0 : j0 + width])
    picked[...] = sums.astype(BF16)
    for k0 in range(0, slots, FWD):
        rows = picked[pl.ds(k0, FWD), :]
        forward_step(k0, [rows * own for own in own_row])
    proj_parts[my_slab] = scatter_tiles(fwd[...] * live[...])
    proj_copies = slab_exchange(proj_parts, proj_send, proj_recv)

    block_id = lax.broadcasted_iota(jnp.int32, (kept, width), 0)

    def live_left(k, ids):
        row = jnp.broadcast_to(live[k : k + 1, :], (kept, width))
        left = jnp.where(ids == voxel_s[0, k], row, 0.0).astype(BF16)
        left_live[k] = left
        return left

    def residual_left(k, ids):
        row = jnp.broadcast_to(fwd[k : k + 1, :], (kept, width))
        return left_live[k] * row.astype(BF16)

    def backward(left_of, out_ref):
        totals = []
        shares = []
        for g in range(groups):
            share = lax.div(voxel_s[0, g * cap], kept)
            ids = block_id + share * kept
            total = jnp.zeros((kept, width), F32)
            for k0 in range(g * cap, (g + 1) * cap, BWD):
                cols = [left_of(k, ids) for k in range(k0, k0 + BWD)]
                mats = w[pl.ds(k0, BWD)].reshape(BWD * width, width)
                total = total + dot(jnp.concatenate(cols, axis=1), mats)
            totals.append(total)
            shares.append(jnp.full((kept, width), share, jnp.int32))
        for s in range(n_angle):
            out = jnp.where(shares[0] == s, totals[0], 0.0)
            for g in range(1, groups):
                out = jnp.where(shares[g] == s, totals[g], out)
            out_ref[s] = out

    backward(live_left, col_out)
    col_copies = angle_exchange(col_out, col_in, col_send, col_recv)

    meas_copy.wait()
    for c in row_copies:
        c.wait()
    row_sum = row_parts[0]
    for s in range(1, n_slab):
        row_sum = row_sum + row_parts[s]
    row_sum = jnp.maximum(row_sum, 1.0)
    for c in proj_copies:
        c.wait()
    proj = proj_parts[0]
    for s in range(1, n_slab):
        proj = proj + proj_parts[s]
    weighted = (meas[...] - proj) / row_sum
    res_buf[...] = weighted
    res_copy = pltpu.make_async_copy(res_buf, res_hbm, out_sem.at[0])
    res_copy.start()
    sel = jnp.where(tile_col == lane, 1.0, 0.0)[:, :tiles].astype(BF16)
    fwd[...] = dot(sel, weighted.astype(BF16))
    backward(residual_left, back_out)
    back_copies = angle_exchange(back_out, back_in, back_send, back_recv)

    back_in[my_angle] = back_out[my_angle]
    col_in[my_angle] = col_out[my_angle]
    for c in col_copies:
        c.wait()
    col_sum = col_in[0]
    for s in range(1, n_angle):
        col_sum = col_sum + col_in[s]
    col_sum = jnp.maximum(col_sum, 1.0)
    for c in back_copies:
        c.wait_recv()
    back = back_in[0]
    for s in range(1, n_angle):
        back = back + back_in[s]
    new_buf[...] = back / col_sum
    new_copy = pltpu.make_async_copy(new_buf, new_hbm, out_sem.at[1])
    new_copy.start()
    for c in vals_copies:
        c.wait_send()
    for c in back_copies:
        c.wait_send()
    res_copy.wait()
    new_copy.wait()


def on_device(volume, measured, footprint, block_voxel, block_tile, block_rows):
    n_slab = lax.axis_size("slab")
    n_angle = lax.axis_size("angle")
    kept, width = volume.shape
    tiles = measured.shape[0]
    slots = footprint.shape[0]
    cap = 2 * slots // n_angle
    any_space = pl.BlockSpec(memory_space=pl.ANY)
    dma = pltpu.SemaphoreType.DMA
    index = pltpu.VMEM((1, slots), jnp.int32)
    per_share = pltpu.VMEM((n_angle, kept, width), F32)
    per_slab = pltpu.VMEM((n_slab, tiles, width), F32)
    by_slot = pltpu.VMEM((slots, width), F32)
    new, res = pl.pallas_call(
        functools.partial(kernel, n_slab, n_angle, cap),
        out_shape=(
            jax.ShapeDtypeStruct(volume.shape, F32),
            jax.ShapeDtypeStruct(measured.shape, F32),
        ),
        in_specs=[any_space] * 6,
        out_specs=(any_space, any_space),
        scratch_shapes=[
            pltpu.VMEM(footprint.shape, BF16),
            pltpu.VMEM(footprint.shape, BF16),
            pltpu.VMEM(volume.shape, F32),
            pltpu.VMEM(measured.shape, F32),
            index, index, index,
            pltpu.SMEM((1, slots), jnp.int32),
            pltpu.VMEM((n_angle, kept, width), BF16),
            pltpu.VMEM((slots, width), BF16),
            by_slot, by_slot,
            pltpu.VMEM((tiles, slots), BF16),
            per_slab, per_slab,
            per_share, per_share, per_share, per_share,
            pltpu.VMEM(measured.shape, F32),
            pltpu.VMEM(volume.shape, F32),
            pltpu.VMEM((slots, kept, width), BF16),
            dma((PIECES,)), dma((6,)), dma((2,)),
            dma((n_angle - 1,)), dma((n_angle - 1,)),
            dma((n_slab - 1,)), dma((n_slab - 1,)),
            dma((n_slab - 1,)), dma((n_slab - 1,)),
            dma((n_angle - 1,)), dma((n_angle - 1,)),
            dma((n_angle - 1,)), dma((n_angle - 1,)),
        ],
        compiler_params=pltpu.CompilerParams(
            collective_id=0, has_side_effects=True, vmem_limit_bytes=56 * 1024 * 1024
        ),
        cost_estimate=pl.CostEstimate(
            flops=8 * slots * width * width, bytes_accessed=2 * slots * width * width, transcendentals=0
        ),
    )(
        volume, measured, footprint,
        block_voxel.reshape(1, slots), block_tile.reshape(1, slots), block_rows.reshape(1, slots),
    )
    return volume + new, res


def solution(mesh):
    in_specs = (
        P(("slab", "angle"), None),
        P("angle", None),
        P(("slab", "angle"), None, None),
        P(("slab", "angle")),
        P(("slab", "angle")),
        P(("slab", "angle")),
    )
    out_specs = (P(("slab", "angle"), None), P("angle", None))
    return jax.shard_map(
        on_device, mesh=mesh, in_specs=in_specs, out_specs=out_specs, check_vma=False
    )
```

```python
import functools

import jax
import jax.numpy as jnp
from jax import lax
from jax.experimental import pallas as pl
from jax.experimental.pallas import tpu as pltpu
from jax.sharding import PartitionSpec as P

MESH = pl.DeviceIdType.MESH
F32 = jnp.float32
BF16 = jnp.bfloat16
FWD = 16
BWD = 12
PIECES = 4


def dot(a, b):
    return jnp.dot(a, b, preferred_element_type=F32)


def three_terms(x):
    hi = x.astype(BF16)
    rest = x - hi.astype(F32)
    mid = rest.astype(BF16)
    lo = (rest - mid.astype(F32)).astype(BF16)
    return hi, mid, lo


def kernel(
    n_slab, n_angle, cap,
    vol_hbm, meas_hbm, foot_hbm, voxel_hbm, tile_hbm, rows_hbm,
    new_hbm, res_hbm,
    w, w_turned, vol, meas, voxel_v, tile_v, rows_v, voxel_s,
    slab_vals, picked, live, fwd, onehot_t, row_parts, proj_parts,
    col_out, col_in, back_out, back_in, res_buf, new_buf, left_live,
    piece_sem, local_sem, out_sem,
    vals_send, vals_recv, row_send, row_recv, proj_send, proj_recv,
    col_send, col_recv, back_send, back_recv,
):
    slots, width, _ = w.shape
    kept = vol.shape[0]
    tiles = meas.shape[0]
    groups = slots // cap
    piece = slots // PIECES
    my_slab = lax.axis_index("slab")
    my_angle = lax.axis_index("angle")

    far_first = sorted(range(1, n_angle), key=lambda d: -min(d, n_angle - d))

    def angle_peer(d):
        return lax.rem(my_angle + d, n_angle)

    def slab_peer(d):
        return lax.rem(my_slab + d, n_slab)

    vol_copy = pltpu.make_async_copy(vol_hbm, vol, local_sem.at[0])
    vol_copy.start()
    index_copies = [
        pltpu.make_async_copy(voxel_hbm, voxel_v, local_sem.at[1]),
        pltpu.make_async_copy(tile_hbm, tile_v, local_sem.at[2]),
        pltpu.make_async_copy(rows_hbm, rows_v, local_sem.at[3]),
        pltpu.make_async_copy(voxel_hbm, voxel_s, local_sem.at[4]),
    ]
    for c in index_copies:
        c.start()
    piece_copies = []
    for i in range(PIECES):
        span = pl.ds(i * piece, piece)
        c = pltpu.make_async_copy(foot_hbm.at[span], w.at[span], piece_sem.at[i])
        c.start()
        piece_copies.append(c)
    meas_copy = pltpu.make_async_copy(meas_hbm, meas, local_sem.at[5])
    meas_copy.start()

    barrier = pltpu.get_barrier_semaphore()
    for d in range(1, n_angle):
        pl.semaphore_signal(barrier, inc=1, device_id={"angle": angle_peer(d)}, device_id_type=MESH)
    for d in range(1, n_slab):
        pl.semaphore_signal(barrier, inc=1, device_id={"slab": slab_peer(d)}, device_id_type=MESH)
    vol_copy.wait()
    slab_vals[my_angle] = vol[...].astype(BF16)
    pl.semaphore_wait(barrier, n_angle + n_slab - 2)

    vals_copies = []
    for d in far_first:
        c = pltpu.make_async_remote_copy(
            src_ref=slab_vals.at[my_angle], dst_ref=slab_vals.at[my_angle],
            send_sem=vals_send.at[d - 1], recv_sem=vals_recv.at[d - 1],
            device_id={"angle": angle_peer(d)}, device_id_type=MESH,
        )
        c.start()
        vals_copies.append(c)

    def slab_exchange(buf, send, recv):
        copies = []
        for d in range(1, n_slab):
            c = pltpu.make_async_remote_copy(
                src_ref=buf.at[my_slab], dst_ref=buf.at[my_slab],
                send_sem=send.at[d - 1], recv_sem=recv.at[d - 1],
                device_id={"slab": slab_peer(d)}, device_id_type=MESH,
            )
            c.start()
            copies.append(c)
        return copies

    def angle_exchange(out, into, send, recv):
        copies = []
        for d in far_first:
            c = pltpu.make_async_remote_copy(
                src_ref=out.at[angle_peer(d)], dst_ref=into.at[my_angle],
                send_sem=send.at[d - 1], recv_sem=recv.at[d - 1],
                device_id={"angle": angle_peer(d)}, device_id_type=MESH,
            )
            c.start()
            copies.append(c)
        return copies

    for c in index_copies:
        c.wait()

    def down(ref):
        return jnp.broadcast_to(ref[...].astype(F32), (width, slots)).T

    voxel_col = down(voxel_v)
    tile_col = down(tile_v)
    lane = lax.broadcasted_iota(jnp.int32, (slots, width), 1).astype(F32)
    live[...] = jnp.where(lane < down(rows_v), 1.0, 0.0)
    tile_rows = lax.broadcasted_iota(jnp.int32, (tiles, slots), 0)
    onehot_t[...] = jnp.where(tile_rows == tile_v[...], 1.0, 0.0).astype(BF16)

    def scatter_tiles(values):
        terms = jnp.concatenate(three_terms(values), axis=1)
        out = dot(onehot_t[...], terms)
        return (out[:, 2 * width :] + out[:, width : 2 * width]) + out[:, :width]

    row_id = lax.broadcasted_iota(jnp.int32, (FWD, width), 0)
    own_row = [jnp.where(row_id == i, 1.0, 0.0).astype(BF16) for i in range(FWD)]

    def forward_step(k0, left):
        mats = w_turned[pl.ds(k0, FWD)].reshape(FWD * width, width)
        fwd[pl.ds(k0, FWD), :] = dot(jnp.concatenate(left, axis=1), mats)

    for i in range(PIECES):
        piece_copies[i].wait()
        for k0 in range(i * piece, (i + 1) * piece, FWD):
            for k in range(k0, k0 + FWD):
                w_turned[k] = w[k].T
            forward_step(k0, own_row)
    row_parts[my_slab] = scatter_tiles(fwd[...] * live[...])
    row_copies = slab_exchange(row_parts, row_send, row_recv)

    for c in vals_copies:
        c.wait_recv()
    all_vals = slab_vals[...].reshape(n_angle * kept, width)
    sums = jnp.zeros((slots, width), F32)
    for j0 in range(0, n_angle * kept, width):
        sel = jnp.where(voxel_col == lane + float(j0), 1.0, 0.0).astype(BF16)
        sums = sums + dot(sel, all_vals[j0 : j0 + width])
    picked[...] = sums.astype(BF16)
    for k0 in range(0, slots, FWD):
        rows = picked[pl.ds(k0, FWD), :]
        forward_step(k0, [rows * own for own in own_row])
    proj_parts[my_slab] = scatter_tiles(fwd[...] * live[...])
    proj_copies = slab_exchange(proj_parts, proj_send, proj_recv)

    block_id = lax.broadcasted_iota(jnp.int32, (kept, width), 0)

    def live_left(k, ids):
        row = jnp.broadcast_to(live[k : k + 1, :], (kept, width))
        left = jnp.where(ids == voxel_s[0, k], row, 0.0).astype(BF16)
        left_live[k] = left
        return left

    def live_sums(out_ref):
        totals = []
        shares = []
        for g in range(groups):
            share = lax.div(voxel_s[0, g * cap], kept)
            ids = block_id + share * kept
            total = jnp.zeros((kept, width), F32)
            for k0 in range(g * cap, (g + 1) * cap, BWD):
                cols = [live_left(k, ids) for k in range(k0, k0 + BWD)]
                mats = w[pl.ds(k0, BWD)].reshape(BWD * width, width)
                total = total + dot(jnp.concatenate(cols, axis=1), mats)
            totals.append(total)
            shares.append(jnp.full((kept, width), share, jnp.int32))
        for s in range(n_angle):
            out = jnp.where(shares[0] == s, totals[0], 0.0)
            for g in range(1, groups):
                out = jnp.where(shares[g] == s, totals[g], out)
            out_ref[s] = out

    live_sums(col_out)
    col_copies = angle_exchange(col_out, col_in, col_send, col_recv)

    meas_copy.wait()
    for c in row_copies:
        c.wait()
    row_sum = row_parts[0]
    for s in range(1, n_slab):
        row_sum = row_sum + row_parts[s]
    row_sum = jnp.maximum(row_sum, 1.0)
    for c in proj_copies:
        c.wait()
    proj = proj_parts[0]
    for s in range(1, n_slab):
        proj = proj + proj_parts[s]
    weighted = (meas[...] - proj) / row_sum
    res_buf[...] = weighted
    res_copy = pltpu.make_async_copy(res_buf, res_hbm, out_sem.at[0])
    res_copy.start()
    sel = jnp.where(tile_col == lane, 1.0, 0.0)[:, :tiles].astype(BF16)
    fwd[...] = dot(sel, weighted.astype(BF16))
    group_shares = [lax.div(voxel_s[0, g * cap], kept) for g in range(groups)]

    def residual_sums(share):
        first = jnp.int32(0)
        named = jnp.float32(0.0)
        for g in range(groups):
            here = group_shares[g] == share
            first = jnp.where(here, g * cap, first)
            named = jnp.where(here, 1.0, named)
        total = jnp.zeros((kept, width), F32)
        for k0 in range(0, cap, BWD):
            cols = []
            for k in range(k0, k0 + BWD):
                row = jnp.broadcast_to(fwd[pl.ds(first + k, 1), :], (kept, width))
                cols.append(left_live[first + k] * row.astype(BF16))
            mats = w[pl.ds(first + k0, BWD)].reshape(BWD * width, width)
            total = total + dot(jnp.concatenate(cols, axis=1), mats)
        return total * named

    back_copies = []
    for d in far_first:
        back_out[d] = residual_sums(angle_peer(d))
        c = pltpu.make_async_remote_copy(
            src_ref=back_out.at[d], dst_ref=back_in.at[my_angle],
            send_sem=back_send.at[d - 1], recv_sem=back_recv.at[d - 1],
            device_id={"angle": angle_peer(d)}, device_id_type=MESH,
        )
        c.start()
        back_copies.append(c)
    back_in[my_angle] = residual_sums(my_angle)

    col_in[my_angle] = col_out[my_angle]
    for c in col_copies:
        c.wait()
    col_sum = col_in[0]
    for s in range(1, n_angle):
        col_sum = col_sum + col_in[s]
    col_sum = jnp.maximum(col_sum, 1.0)
    for c in back_copies:
        c.wait_recv()
    back = back_in[0]
    for s in range(1, n_angle):
        back = back + back_in[s]
    new_buf[...] = back / col_sum
    new_copy = pltpu.make_async_copy(new_buf, new_hbm, out_sem.at[1])
    new_copy.start()
    for c in vals_copies:
        c.wait_send()
    for c in back_copies:
        c.wait_send()
    res_copy.wait()
    new_copy.wait()


def on_device(volume, measured, footprint, block_voxel, block_tile, block_rows):
    n_slab = lax.axis_size("slab")
    n_angle = lax.axis_size("angle")
    kept, width = volume.shape
    tiles = measured.shape[0]
    slots = footprint.shape[0]
    cap = 2 * slots // n_angle
    any_space = pl.BlockSpec(memory_space=pl.ANY)
    dma = pltpu.SemaphoreType.DMA
    index = pltpu.VMEM((1, slots), jnp.int32)
    per_share = pltpu.VMEM((n_angle, kept, width), F32)
    per_slab = pltpu.VMEM((n_slab, tiles, width), F32)
    by_slot = pltpu.VMEM((slots, width), F32)
    new, res = pl.pallas_call(
        functools.partial(kernel, n_slab, n_angle, cap),
        out_shape=(
            jax.ShapeDtypeStruct(volume.shape, F32),
            jax.ShapeDtypeStruct(measured.shape, F32),
        ),
        in_specs=[any_space] * 6,
        out_specs=(any_space, any_space),
        scratch_shapes=[
            pltpu.VMEM(footprint.shape, BF16),
            pltpu.VMEM(footprint.shape, BF16),
            pltpu.VMEM(volume.shape, F32),
            pltpu.VMEM(measured.shape, F32),
            index, index, index,
            pltpu.SMEM((1, slots), jnp.int32),
            pltpu.VMEM((n_angle, kept, width), BF16),
            pltpu.VMEM((slots, width), BF16),
            by_slot, by_slot,
            pltpu.VMEM((tiles, slots), BF16),
            per_slab, per_slab,
            per_share, per_share, per_share, per_share,
            pltpu.VMEM(measured.shape, F32),
            pltpu.VMEM(volume.shape, F32),
            pltpu.VMEM((slots, kept, width), BF16),
            dma((PIECES,)), dma((6,)), dma((2,)),
            dma((n_angle - 1,)), dma((n_angle - 1,)),
            dma((n_slab - 1,)), dma((n_slab - 1,)),
            dma((n_slab - 1,)), dma((n_slab - 1,)),
            dma((n_angle - 1,)), dma((n_angle - 1,)),
            dma((n_angle - 1,)), dma((n_angle - 1,)),
        ],
        compiler_params=pltpu.CompilerParams(
            collective_id=0, has_side_effects=True, vmem_limit_bytes=56 * 1024 * 1024
        ),
        cost_estimate=pl.CostEstimate(
            flops=8 * slots * width * width, bytes_accessed=2 * slots * width * width, transcendentals=0
        ),
    )(
        volume, measured, footprint,
        block_voxel.reshape(1, slots), block_tile.reshape(1, slots), block_rows.reshape(1, slots),
    )
    return volume + new, res


def solution(mesh):
    in_specs = (
        P(("slab", "angle"), None),
        P("angle", None),
        P(("slab", "angle"), None, None),
        P(("slab", "angle")),
        P(("slab", "angle")),
        P(("slab", "angle")),
    )
    out_specs = (P(("slab", "angle"), None), P("angle", None))
    return jax.shard_map(
        on_device, mesh=mesh, in_specs=in_specs, out_specs=out_specs, check_vma=False
    )
```

```python
import functools

import jax
import jax.numpy as jnp
from jax import lax
from jax.experimental import pallas as pl
from jax.experimental.pallas import tpu as pltpu
from jax.sharding import PartitionSpec as P

MESH = pl.DeviceIdType.MESH
F32 = jnp.float32
BF16 = jnp.bfloat16
FWD = 16
BWD = 6
PIECES = 4


def dot(a, b):
    return jnp.dot(a, b, preferred_element_type=F32)


def three_terms(x):
    hi = x.astype(BF16)
    rest = x - hi.astype(F32)
    mid = rest.astype(BF16)
    lo = (rest - mid.astype(F32)).astype(BF16)
    return hi, mid, lo


def kernel(
    n_slab, n_angle, cap,
    vol_hbm, meas_hbm, foot_hbm, voxel_hbm, tile_hbm, rows_hbm,
    new_hbm, res_hbm,
    w, w_turned, vol, meas, voxel_v, tile_v, rows_v, voxel_s,
    slab_vals, picked, live, fwd, onehot_t, row_parts, proj_parts,
    col_out, col_in, back_out, back_in, res_buf, new_buf, left_live,
    piece_sem, local_sem, out_sem,
    vals_send, vals_recv, row_send, row_recv, proj_send, proj_recv,
    col_send, col_recv, back_send, back_recv,
):
    slots, width, _ = w.shape
    kept = vol.shape[0]
    tiles = meas.shape[0]
    groups = slots // cap
    piece = slots // PIECES
    my_slab = lax.axis_index("slab")
    my_angle = lax.axis_index("angle")

    far_first = sorted(range(1, n_angle), key=lambda d: -min(d, n_angle - d))

    def angle_peer(d):
        return lax.rem(my_angle + d, n_angle)

    def slab_peer(d):
        return lax.rem(my_slab + d, n_slab)

    vol_copy = pltpu.make_async_copy(vol_hbm, vol, local_sem.at[0])
    vol_copy.start()
    index_copies = [
        pltpu.make_async_copy(voxel_hbm, voxel_v, local_sem.at[1]),
        pltpu.make_async_copy(tile_hbm, tile_v, local_sem.at[2]),
        pltpu.make_async_copy(rows_hbm, rows_v, local_sem.at[3]),
        pltpu.make_async_copy(voxel_hbm, voxel_s, local_sem.at[4]),
    ]
    for c in index_copies:
        c.start()
    piece_copies = []
    for i in range(PIECES):
        span = pl.ds(i * piece, piece)
        c = pltpu.make_async_copy(foot_hbm.at[span], w.at[span], piece_sem.at[i])
        c.start()
        piece_copies.append(c)
    meas_copy = pltpu.make_async_copy(meas_hbm, meas, local_sem.at[5])
    meas_copy.start()

    barrier = pltpu.get_barrier_semaphore()
    for d in range(1, n_angle):
        pl.semaphore_signal(barrier, inc=1, device_id={"angle": angle_peer(d)}, device_id_type=MESH)
    for d in range(1, n_slab):
        pl.semaphore_signal(barrier, inc=1, device_id={"slab": slab_peer(d)}, device_id_type=MESH)
    vol_copy.wait()
    slab_vals[my_angle] = vol[...].astype(BF16)
    pl.semaphore_wait(barrier, n_angle + n_slab - 2)

    vals_copies = []
    for d in far_first:
        c = pltpu.make_async_remote_copy(
            src_ref=slab_vals.at[my_angle], dst_ref=slab_vals.at[my_angle],
            send_sem=vals_send.at[d - 1], recv_sem=vals_recv.at[d - 1],
            device_id={"angle": angle_peer(d)}, device_id_type=MESH,
        )
        c.start()
        vals_copies.append(c)

    def slab_exchange(buf, send, recv):
        copies = []
        for d in range(1, n_slab):
            c = pltpu.make_async_remote_copy(
                src_ref=buf.at[my_slab], dst_ref=buf.at[my_slab],
                send_sem=send.at[d - 1], recv_sem=recv.at[d - 1],
                device_id={"slab": slab_peer(d)}, device_id_type=MESH,
            )
            c.start()
            copies.append(c)
        return copies

    def angle_exchange(out, into, send, recv):
        copies = []
        for d in far_first:
            c = pltpu.make_async_remote_copy(
                src_ref=out.at[angle_peer(d)], dst_ref=into.at[my_angle],
                send_sem=send.at[d - 1], recv_sem=recv.at[d - 1],
                device_id={"angle": angle_peer(d)}, device_id_type=MESH,
            )
            c.start()
            copies.append(c)
        return copies

    for c in index_copies:
        c.wait()

    def down(ref):
        return jnp.broadcast_to(ref[...].astype(F32), (width, slots)).T

    voxel_col = down(voxel_v)
    tile_col = down(tile_v)
    lane = lax.broadcasted_iota(jnp.int32, (slots, width), 1).astype(F32)
    live[...] = jnp.where(lane < down(rows_v), 1.0, 0.0)
    tile_rows = lax.broadcasted_iota(jnp.int32, (tiles, slots), 0)
    onehot_t[...] = jnp.where(tile_rows == tile_v[...], 1.0, 0.0).astype(BF16)

    def scatter_tiles(values):
        terms = jnp.concatenate(three_terms(values), axis=1)
        out = dot(onehot_t[...], terms)
        return (out[:, 2 * width :] + out[:, width : 2 * width]) + out[:, :width]

    row_id = lax.broadcasted_iota(jnp.int32, (FWD, width), 0)
    half = FWD // 2
    own_row = [
        jnp.where((row_id == i) | (row_id == i + half), 1.0, 0.0).astype(BF16) for i in range(half)
    ]

    def side_by_side(ref, k0, count):
        return jnp.concatenate(
            [ref[pl.ds(k, count)].reshape(count * width, width) for k in (k0, k0 + count)], axis=1
        )

    def forward_step(k0, left):
        prod = dot(jnp.concatenate(left, axis=1), side_by_side(w_turned, k0, half))
        fwd[pl.ds(k0, half), :] = prod[:half, :width]
        fwd[pl.ds(k0 + half, half), :] = prod[half:, width:]

    for i in range(PIECES):
        piece_copies[i].wait()
        for k0 in range(i * piece, (i + 1) * piece, FWD):
            for k in range(k0, k0 + FWD):
                w_turned[k] = w[k].T
            forward_step(k0, own_row)
    row_parts[my_slab] = scatter_tiles(fwd[...] * live[...])
    row_copies = slab_exchange(row_parts, row_send, row_recv)

    for c in vals_copies:
        c.wait_recv()
    all_vals = slab_vals[...].reshape(n_angle * kept, width)
    sums = jnp.zeros((slots, width), F32)
    for j0 in range(0, n_angle * kept, width):
        sel = jnp.where(voxel_col == lane + float(j0), 1.0, 0.0).astype(BF16)
        sums = sums + dot(sel, all_vals[j0 : j0 + width])
    picked[...] = sums.astype(BF16)
    for k0 in range(0, slots, FWD):
        rows = picked[pl.ds(k0, FWD), :]
        forward_step(k0, [rows * own for own in own_row])
    proj_parts[my_slab] = scatter_tiles(fwd[...] * live[...])
    proj_copies = slab_exchange(proj_parts, proj_send, proj_recv)

    block_id = lax.broadcasted_iota(jnp.int32, (kept, width), 0)

    def live_left(k, ids):
        row = jnp.broadcast_to(live[k : k + 1, :], (kept, width))
        left = jnp.where(ids == voxel_s[0, k], row, 0.0).astype(BF16)
        left_live[k] = left
        return left

    def residual_left(k, ids):
        row = jnp.broadcast_to(fwd[k : k + 1, :], (kept, width))
        return left_live[k] * row.astype(BF16)

    def backward(left_of, out_ref):
        totals = []
        shares = []
        for g in range(groups):
            share = lax.div(voxel_s[0, g * cap], kept)
            ids = block_id + share * kept
            total = jnp.zeros((kept, width), F32)
            for k0 in range(g * cap, (g + 1) * cap, 2 * BWD):
                left = [
                    jnp.concatenate([left_of(k + i, ids) for i in range(BWD)], axis=1)
                    for k in (k0, k0 + BWD)
                ]
                prod = dot(jnp.concatenate(left, axis=0), side_by_side(w, k0, BWD))
                total = total + (prod[:kept, :width] + prod[kept:, width:])
            totals.append(total)
            shares.append(jnp.full((kept, width), share, jnp.int32))
        for s in range(n_angle):
            out = jnp.where(shares[0] == s, totals[0], 0.0)
            for g in range(1, groups):
                out = jnp.where(shares[g] == s, totals[g], out)
            out_ref[s] = out

    backward(live_left, col_out)
    col_copies = angle_exchange(col_out, col_in, col_send, col_recv)

    meas_copy.wait()
    for c in row_copies:
        c.wait()
    row_sum = row_parts[0]
    for s in range(1, n_slab):
        row_sum = row_sum + row_parts[s]
    row_sum = jnp.maximum(row_sum, 1.0)
    for c in proj_copies:
        c.wait()
    proj = proj_parts[0]
    for s in range(1, n_slab):
        proj = proj + proj_parts[s]
    weighted = (meas[...] - proj) / row_sum
    res_buf[...] = weighted
    res_copy = pltpu.make_async_copy(res_buf, res_hbm, out_sem.at[0])
    res_copy.start()
    sel = jnp.where(tile_col == lane, 1.0, 0.0)[:, :tiles].astype(BF16)
    fwd[...] = dot(sel, weighted.astype(BF16))
    backward(residual_left, back_out)
    back_copies = angle_exchange(back_out, back_in, back_send, back_recv)

    back_in[my_angle] = back_out[my_angle]
    col_in[my_angle] = col_out[my_angle]
    for c in col_copies:
        c.wait()
    col_sum = col_in[0]
    for s in range(1, n_angle):
        col_sum = col_sum + col_in[s]
    col_sum = jnp.maximum(col_sum, 1.0)
    for c in back_copies:
        c.wait_recv()
    back = back_in[0]
    for s in range(1, n_angle):
        back = back + back_in[s]
    new_buf[...] = back / col_sum
    new_copy = pltpu.make_async_copy(new_buf, new_hbm, out_sem.at[1])
    new_copy.start()
    for c in vals_copies:
        c.wait_send()
    for c in back_copies:
        c.wait_send()
    res_copy.wait()
    new_copy.wait()


def on_device(volume, measured, footprint, block_voxel, block_tile, block_rows):
    n_slab = lax.axis_size("slab")
    n_angle = lax.axis_size("angle")
    kept, width = volume.shape
    tiles = measured.shape[0]
    slots = footprint.shape[0]
    cap = 2 * slots // n_angle
    any_space = pl.BlockSpec(memory_space=pl.ANY)
    dma = pltpu.SemaphoreType.DMA
    index = pltpu.VMEM((1, slots), jnp.int32)
    per_share = pltpu.VMEM((n_angle, kept, width), F32)
    per_slab = pltpu.VMEM((n_slab, tiles, width), F32)
    by_slot = pltpu.VMEM((slots, width), F32)
    new, res = pl.pallas_call(
        functools.partial(kernel, n_slab, n_angle, cap),
        out_shape=(
            jax.ShapeDtypeStruct(volume.shape, F32),
            jax.ShapeDtypeStruct(measured.shape, F32),
        ),
        in_specs=[any_space] * 6,
        out_specs=(any_space, any_space),
        scratch_shapes=[
            pltpu.VMEM(footprint.shape, BF16),
            pltpu.VMEM(footprint.shape, BF16),
            pltpu.VMEM(volume.shape, F32),
            pltpu.VMEM(measured.shape, F32),
            index, index, index,
            pltpu.SMEM((1, slots), jnp.int32),
            pltpu.VMEM((n_angle, kept, width), BF16),
            pltpu.VMEM((slots, width), BF16),
            by_slot, by_slot,
            pltpu.VMEM((tiles, slots), BF16),
            per_slab, per_slab,
            per_share, per_share, per_share, per_share,
            pltpu.VMEM(measured.shape, F32),
            pltpu.VMEM(volume.shape, F32),
            pltpu.VMEM((slots, kept, width), BF16),
            dma((PIECES,)), dma((6,)), dma((2,)),
            dma((n_angle - 1,)), dma((n_angle - 1,)),
            dma((n_slab - 1,)), dma((n_slab - 1,)),
            dma((n_slab - 1,)), dma((n_slab - 1,)),
            dma((n_angle - 1,)), dma((n_angle - 1,)),
            dma((n_angle - 1,)), dma((n_angle - 1,)),
        ],
        compiler_params=pltpu.CompilerParams(
            collective_id=0, has_side_effects=True, vmem_limit_bytes=56 * 1024 * 1024
        ),
        cost_estimate=pl.CostEstimate(
            flops=8 * slots * width * width, bytes_accessed=2 * slots * width * width, transcendentals=0
        ),
    )(
        volume, measured, footprint,
        block_voxel.reshape(1, slots), block_tile.reshape(1, slots), block_rows.reshape(1, slots),
    )
    return volume + new, res


def solution(mesh):
    in_specs = (
        P(("slab", "angle"), None),
        P("angle", None),
        P(("slab", "angle"), None, None),
        P(("slab", "angle")),
        P(("slab", "angle")),
        P(("slab", "angle")),
    )
    out_specs = (P(("slab", "angle"), None), P("angle", None))
    return jax.shard_map(
        on_device, mesh=mesh, in_specs=in_specs, out_specs=out_specs, check_vma=False
    )
```

```python
import functools

import jax
import jax.numpy as jnp
from jax import lax
from jax.experimental import pallas as pl
from jax.experimental.pallas import tpu as pltpu
from jax.sharding import PartitionSpec as P

MESH = pl.DeviceIdType.MESH
F32 = jnp.float32
BF16 = jnp.bfloat16
FWD = 16
BWD = 6
PIECES = 4


def dot(a, b):
    return jnp.dot(a, b, preferred_element_type=F32)


def three_terms(x):
    hi = x.astype(BF16)
    rest = x - hi.astype(F32)
    mid = rest.astype(BF16)
    lo = (rest - mid.astype(F32)).astype(BF16)
    return hi, mid, lo


def kernel(
    n_slab, n_angle, cap,
    vol_hbm, meas_hbm, foot_hbm, voxel_hbm, tile_hbm, rows_hbm,
    new_hbm, res_hbm,
    w, w_turned, vol, meas, voxel_v, tile_v, rows_v, voxel_s,
    slab_vals, picked, live, fwd, onehot_t, row_parts, proj_parts,
    col_out, col_in, back_out, back_in, res_buf, new_buf, left_live,
    piece_sem, local_sem, out_sem,
    vals_send, vals_recv, row_send, row_recv, proj_send, proj_recv,
    col_send, col_recv, back_send, back_recv,
):
    slots, width, _ = w.shape
    kept = vol.shape[0]
    tiles = meas.shape[0]
    groups = slots // cap
    piece = slots // PIECES
    my_slab = lax.axis_index("slab")
    my_angle = lax.axis_index("angle")

    far_first = range(n_angle - 1, 0, -1)

    def angle_peer(d):
        if n_angle & (n_angle - 1):
            return lax.rem(my_angle + d, n_angle)
        peer = my_angle
        bit = 1
        while bit < n_angle:
            if d & bit:
                peer = peer + bit * (1 - 2 * lax.rem(lax.div(my_angle, bit), 2))
            bit *= 2
        return peer

    def slab_peer(d):
        return lax.rem(my_slab + d, n_slab)

    vol_copy = pltpu.make_async_copy(vol_hbm, vol, local_sem.at[0])
    vol_copy.start()
    index_copies = [
        pltpu.make_async_copy(voxel_hbm, voxel_v, local_sem.at[1]),
        pltpu.make_async_copy(tile_hbm, tile_v, local_sem.at[2]),
        pltpu.make_async_copy(rows_hbm, rows_v, local_sem.at[3]),
        pltpu.make_async_copy(voxel_hbm, voxel_s, local_sem.at[4]),
    ]
    for c in index_copies:
        c.start()
    piece_copies = []
    for i in range(PIECES):
        span = pl.ds(i * piece, piece)
        c = pltpu.make_async_copy(foot_hbm.at[span], w.at[span], piece_sem.at[i])
        c.start()
        piece_copies.append(c)
    meas_copy = pltpu.make_async_copy(meas_hbm, meas, local_sem.at[5])
    meas_copy.start()

    barrier = pltpu.get_barrier_semaphore()
    for d in range(1, n_angle):
        pl.semaphore_signal(barrier, inc=1, device_id={"angle": angle_peer(d)}, device_id_type=MESH)
    for d in range(1, n_slab):
        pl.semaphore_signal(barrier, inc=1, device_id={"slab": slab_peer(d)}, device_id_type=MESH)
    vol_copy.wait()
    slab_vals[my_angle] = vol[...].astype(BF16)
    pl.semaphore_wait(barrier, n_angle + n_slab - 2)

    vals_copies = []
    for d in far_first:
        c = pltpu.make_async_remote_copy(
            src_ref=slab_vals.at[my_angle], dst_ref=slab_vals.at[my_angle],
            send_sem=vals_send.at[d - 1], recv_sem=vals_recv.at[d - 1],
            device_id={"angle": angle_peer(d)}, device_id_type=MESH,
        )
        c.start()
        vals_copies.append(c)

    def slab_exchange(buf, send, recv):
        copies = []
        for d in range(1, n_slab):
            c = pltpu.make_async_remote_copy(
                src_ref=buf.at[my_slab], dst_ref=buf.at[my_slab],
                send_sem=send.at[d - 1], recv_sem=recv.at[d - 1],
                device_id={"slab": slab_peer(d)}, device_id_type=MESH,
            )
            c.start()
            copies.append(c)
        return copies

    def angle_exchange(out, into, send, recv):
        copies = []
        for d in far_first:
            c = pltpu.make_async_remote_copy(
                src_ref=out.at[angle_peer(d)], dst_ref=into.at[my_angle],
                send_sem=send.at[d - 1], recv_sem=recv.at[d - 1],
                device_id={"angle": angle_peer(d)}, device_id_type=MESH,
            )
            c.start()
            copies.append(c)
        return copies

    for c in index_copies:
        c.wait()

    def down(ref):
        return jnp.broadcast_to(ref[...].astype(F32), (width, slots)).T

    voxel_col = down(voxel_v)
    tile_col = down(tile_v)
    lane = lax.broadcasted_iota(jnp.int32, (slots, width), 1).astype(F32)
    live[...] = jnp.where(lane < down(rows_v), 1.0, 0.0)
    tile_rows = lax.broadcasted_iota(jnp.int32, (tiles, slots), 0)
    onehot_t[...] = jnp.where(tile_rows == tile_v[...], 1.0, 0.0).astype(BF16)

    def scatter_tiles(values):
        terms = jnp.concatenate(three_terms(values), axis=1)
        out = dot(onehot_t[...], terms)
        return (out[:, 2 * width :] + out[:, width : 2 * width]) + out[:, :width]

    row_id = lax.broadcasted_iota(jnp.int32, (FWD, width), 0)
    half = FWD // 2
    own_row = [
        jnp.where((row_id == i) | (row_id == i + half), 1.0, 0.0).astype(BF16) for i in range(half)
    ]

    def side_by_side(ref, k0, count):
        return jnp.concatenate(
            [ref[pl.ds(k, count)].reshape(count * width, width) for k in (k0, k0 + count)], axis=1
        )

    def forward_step(k0, left):
        prod = dot(jnp.concatenate(left, axis=1), side_by_side(w_turned, k0, half))
        fwd[pl.ds(k0, half), :] = prod[:half, :width]
        fwd[pl.ds(k0 + half, half), :] = prod[half:, width:]

    for i in range(PIECES):
        piece_copies[i].wait()
        for k0 in range(i * piece, (i + 1) * piece, FWD):
            for k in range(k0, k0 + FWD):
                w_turned[k] = w[k].T
            forward_step(k0, own_row)
    row_parts[my_slab] = scatter_tiles(fwd[...] * live[...])
    row_copies = slab_exchange(row_parts, row_send, row_recv)

    for c in vals_copies:
        c.wait_recv()
    all_vals = slab_vals[...].reshape(n_angle * kept, width)
    sums = jnp.zeros((slots, width), F32)
    for j0 in range(0, n_angle * kept, width):
        sel = jnp.where(voxel_col == lane + float(j0), 1.0, 0.0).astype(BF16)
        sums = sums + dot(sel, all_vals[j0 : j0 + width])
    picked[...] = sums.astype(BF16)
    for k0 in range(0, slots, FWD):
        rows = picked[pl.ds(k0, FWD), :]
        forward_step(k0, [rows * own for own in own_row])
    proj_parts[my_slab] = scatter_tiles(fwd[...] * live[...])
    proj_copies = slab_exchange(proj_parts, proj_send, proj_recv)

    block_id = lax.broadcasted_iota(jnp.int32, (kept, width), 0)

    def live_left(k, ids):
        row = jnp.broadcast_to(live[k : k + 1, :], (kept, width))
        left = jnp.where(ids == voxel_s[0, k], row, 0.0).astype(BF16)
        left_live[k] = left
        return left

    def residual_left(k, ids):
        row = jnp.broadcast_to(fwd[k : k + 1, :], (kept, width))
        return left_live[k] * row.astype(BF16)

    def backward(left_of, out_ref):
        totals = []
        shares = []
        for g in range(groups):
            share = lax.div(voxel_s[0, g * cap], kept)
            ids = block_id + share * kept
            total = jnp.zeros((kept, width), F32)
            for k0 in range(g * cap, (g + 1) * cap, 2 * BWD):
                left = [
                    jnp.concatenate([left_of(k + i, ids) for i in range(BWD)], axis=1)
                    for k in (k0, k0 + BWD)
                ]
                prod = dot(jnp.concatenate(left, axis=0), side_by_side(w, k0, BWD))
                total = total + (prod[:kept, :width] + prod[kept:, width:])
            totals.append(total)
            shares.append(jnp.full((kept, width), share, jnp.int32))
        for s in range(n_angle):
            out = jnp.where(shares[0] == s, totals[0], 0.0)
            for g in range(1, groups):
                out = jnp.where(shares[g] == s, totals[g], out)
            out_ref[s] = out

    backward(live_left, col_out)
    col_copies = angle_exchange(col_out, col_in, col_send, col_recv)

    meas_copy.wait()
    for c in row_copies:
        c.wait()
    row_sum = row_parts[0]
    for s in range(1, n_slab):
        row_sum = row_sum + row_parts[s]
    row_sum = jnp.maximum(row_sum, 1.0)
    for c in proj_copies:
        c.wait()
    proj = proj_parts[0]
    for s in range(1, n_slab):
        proj = proj + proj_parts[s]
    weighted = (meas[...] - proj) / row_sum
    res_buf[...] = weighted
    res_copy = pltpu.make_async_copy(res_buf, res_hbm, out_sem.at[0])
    res_copy.start()
    sel = jnp.where(tile_col == lane, 1.0, 0.0)[:, :tiles].astype(BF16)
    fwd[...] = dot(sel, weighted.astype(BF16))
    backward(residual_left, back_out)
    back_copies = angle_exchange(back_out, back_in, back_send, back_recv)

    back_in[my_angle] = back_out[my_angle]
    col_in[my_angle] = col_out[my_angle]
    for c in col_copies:
        c.wait()
    col_sum = col_in[0]
    for s in range(1, n_angle):
        col_sum = col_sum + col_in[s]
    col_sum = jnp.maximum(col_sum, 1.0)
    for c in back_copies:
        c.wait_recv()
    back = back_in[0]
    for s in range(1, n_angle):
        back = back + back_in[s]
    new_buf[...] = back / col_sum
    new_copy = pltpu.make_async_copy(new_buf, new_hbm, out_sem.at[1])
    new_copy.start()
    for c in vals_copies:
        c.wait_send()
    for c in back_copies:
        c.wait_send()
    res_copy.wait()
    new_copy.wait()


def on_device(volume, measured, footprint, block_voxel, block_tile, block_rows):
    n_slab = lax.axis_size("slab")
    n_angle = lax.axis_size("angle")
    kept, width = volume.shape
    tiles = measured.shape[0]
    slots = footprint.shape[0]
    cap = 2 * slots // n_angle
    any_space = pl.BlockSpec(memory_space=pl.ANY)
    dma = pltpu.SemaphoreType.DMA
    index = pltpu.VMEM((1, slots), jnp.int32)
    per_share = pltpu.VMEM((n_angle, kept, width), F32)
    per_slab = pltpu.VMEM((n_slab, tiles, width), F32)
    by_slot = pltpu.VMEM((slots, width), F32)
    new, res = pl.pallas_call(
        functools.partial(kernel, n_slab, n_angle, cap),
        out_shape=(
            jax.ShapeDtypeStruct(volume.shape, F32),
            jax.ShapeDtypeStruct(measured.shape, F32),
        ),
        in_specs=[any_space] * 6,
        out_specs=(any_space, any_space),
        scratch_shapes=[
            pltpu.VMEM(footprint.shape, BF16),
            pltpu.VMEM(footprint.shape, BF16),
            pltpu.VMEM(volume.shape, F32),
            pltpu.VMEM(measured.shape, F32),
            index, index, index,
            pltpu.SMEM((1, slots), jnp.int32),
            pltpu.VMEM((n_angle, kept, width), BF16),
            pltpu.VMEM((slots, width), BF16),
            by_slot, by_slot,
            pltpu.VMEM((tiles, slots), BF16),
            per_slab, per_slab,
            per_share, per_share, per_share, per_share,
            pltpu.VMEM(measured.shape, F32),
            pltpu.VMEM(volume.shape, F32),
            pltpu.VMEM((slots, kept, width), BF16),
            dma((PIECES,)), dma((6,)), dma((2,)),
            dma((n_angle - 1,)), dma((n_angle - 1,)),
            dma((n_slab - 1,)), dma((n_slab - 1,)),
            dma((n_slab - 1,)), dma((n_slab - 1,)),
            dma((n_angle - 1,)), dma((n_angle - 1,)),
            dma((n_angle - 1,)), dma((n_angle - 1,)),
        ],
        compiler_params=pltpu.CompilerParams(
            collective_id=0, has_side_effects=True, vmem_limit_bytes=56 * 1024 * 1024
        ),
        cost_estimate=pl.CostEstimate(
            flops=8 * slots * width * width, bytes_accessed=2 * slots * width * width, transcendentals=0
        ),
    )(
        volume, measured, footprint,
        block_voxel.reshape(1, slots), block_tile.reshape(1, slots), block_rows.reshape(1, slots),
    )
    return volume + new, res


def solution(mesh):
    in_specs = (
        P(("slab", "angle"), None),
        P("angle", None),
        P(("slab", "angle"), None, None),
        P(("slab", "angle")),
        P(("slab", "angle")),
        P(("slab", "angle")),
    )
    out_specs = (P(("slab", "angle"), None), P("angle", None))
    return jax.shard_map(
        on_device, mesh=mesh, in_specs=in_specs, out_specs=out_specs, check_vma=False
    )
```

```python
import functools

import jax
import jax.numpy as jnp
from jax import lax
from jax.experimental import pallas as pl
from jax.experimental.pallas import tpu as pltpu
from jax.sharding import PartitionSpec as P

MESH = pl.DeviceIdType.MESH
F32 = jnp.float32
BF16 = jnp.bfloat16
FWD = 16
BWD = 6
PIECES = 6


def dot(a, b):
    return jnp.dot(a, b, preferred_element_type=F32)


def three_terms(x):
    hi = x.astype(BF16)
    rest = x - hi.astype(F32)
    mid = rest.astype(BF16)
    lo = (rest - mid.astype(F32)).astype(BF16)
    return hi, mid, lo


def kernel(
    n_slab, n_angle, cap,
    vol_hbm, meas_hbm, foot_hbm, voxel_hbm, tile_hbm, rows_hbm,
    new_hbm, res_hbm,
    w, w_turned, vol, meas, voxel_v, tile_v, rows_v, voxel_s,
    slab_vals, picked, live, fwd, onehot_t, row_parts, proj_parts,
    col_out, col_in, back_out, back_in, res_buf, new_buf, left_live,
    piece_sem, local_sem, out_sem,
    vals_send, vals_recv, row_send, row_recv, proj_send, proj_recv,
    col_send, col_recv, back_send, back_recv,
):
    slots, width, _ = w.shape
    kept = vol.shape[0]
    tiles = meas.shape[0]
    groups = slots // cap
    piece = slots // PIECES
    my_slab = lax.axis_index("slab")
    my_angle = lax.axis_index("angle")

    def angle_peer(d):
        return lax.rem(my_angle + d, n_angle)

    def slab_peer(d):
        return lax.rem(my_slab + d, n_slab)

    vol_copy = pltpu.make_async_copy(vol_hbm, vol, local_sem.at[0])
    vol_copy.start()
    barrier = pltpu.get_barrier_semaphore()
    for d in range(1, n_angle):
        pl.semaphore_signal(barrier, inc=1, device_id={"angle": angle_peer(d)}, device_id_type=MESH)
    for d in range(1, n_slab):
        pl.semaphore_signal(barrier, inc=1, device_id={"slab": slab_peer(d)}, device_id_type=MESH)
    index_copies = [
        pltpu.make_async_copy(voxel_hbm, voxel_v, local_sem.at[1]),
        pltpu.make_async_copy(tile_hbm, tile_v, local_sem.at[2]),
        pltpu.make_async_copy(rows_hbm, rows_v, local_sem.at[3]),
        pltpu.make_async_copy(voxel_hbm, voxel_s, local_sem.at[4]),
    ]
    for c in index_copies:
        c.start()
    piece_copies = []
    for i in range(PIECES):
        span = pl.ds(i * piece, piece)
        c = pltpu.make_async_copy(foot_hbm.at[span], w.at[span], piece_sem.at[i])
        c.start()
        piece_copies.append(c)
    meas_copy = pltpu.make_async_copy(meas_hbm, meas, local_sem.at[5])
    meas_copy.start()

    vol_copy.wait()
    slab_vals[my_angle] = vol[...].astype(BF16)
    pl.semaphore_wait(barrier, n_angle + n_slab - 2)

    vals_copies = []
    for d in range(1, n_angle):
        c = pltpu.make_async_remote_copy(
            src_ref=slab_vals.at[my_angle], dst_ref=slab_vals.at[my_angle],
            send_sem=vals_send.at[d - 1], recv_sem=vals_recv.at[d - 1],
            device_id={"angle": angle_peer(d)}, device_id_type=MESH,
        )
        c.start()
        vals_copies.append(c)

    def slab_exchange(buf, send, recv):
        copies = []
        for d in range(1, n_slab):
            c = pltpu.make_async_remote_copy(
                src_ref=buf.at[my_slab], dst_ref=buf.at[my_slab],
                send_sem=send.at[d - 1], recv_sem=recv.at[d - 1],
                device_id={"slab": slab_peer(d)}, device_id_type=MESH,
            )
            c.start()
            copies.append(c)
        return copies

    def angle_exchange(out, into, send, recv):
        copies = []
        for d in range(1, n_angle):
            c = pltpu.make_async_remote_copy(
                src_ref=out.at[angle_peer(d)], dst_ref=into.at[my_angle],
                send_sem=send.at[d - 1], recv_sem=recv.at[d - 1],
                device_id={"angle": angle_peer(d)}, device_id_type=MESH,
            )
            c.start()
            copies.append(c)
        return copies

    for c in index_copies:
        c.wait()

    def down(ref):
        return jnp.broadcast_to(ref[...].astype(F32), (width, slots)).T

    voxel_col = down(voxel_v)
    tile_col = down(tile_v)
    lane = lax.broadcasted_iota(jnp.int32, (slots, width), 1).astype(F32)
    live[...] = jnp.where(lane < down(rows_v), 1.0, 0.0)
    tile_rows = lax.broadcasted_iota(jnp.int32, (tiles, slots), 0)
    onehot_t[...] = jnp.where(tile_rows == tile_v[...], 1.0, 0.0).astype(BF16)

    def scatter_tiles(values):
        terms = jnp.concatenate(three_terms(values), axis=1)
        out = dot(onehot_t[...], terms)
        return (out[:, 2 * width :] + out[:, width : 2 * width]) + out[:, :width]

    row_id = lax.broadcasted_iota(jnp.int32, (FWD, width), 0)
    half = FWD // 2
    own_row = [
        jnp.where((row_id == i) | (row_id == i + half), 1.0, 0.0).astype(BF16) for i in range(half)
    ]

    def side_by_side(ref, k0, count):
        return jnp.concatenate(
            [ref[pl.ds(k, count)].reshape(count * width, width) for k in (k0, k0 + count)], axis=1
        )

    def forward_step(k0, left):
        prod = dot(jnp.concatenate(left, axis=1), side_by_side(w_turned, k0, half))
        fwd[pl.ds(k0, half), :] = prod[:half, :width]
        fwd[pl.ds(k0 + half, half), :] = prod[half:, width:]

    for i in range(PIECES):
        piece_copies[i].wait()
        for k0 in range(i * piece, (i + 1) * piece, FWD):
            for k in range(k0, k0 + FWD):
                w_turned[k] = w[k].T
            forward_step(k0, own_row)
    row_parts[my_slab] = scatter_tiles(fwd[...] * live[...])
    row_copies = slab_exchange(row_parts, row_send, row_recv)

    for c in vals_copies:
        c.wait_recv()
    all_vals = slab_vals[...].reshape(n_angle * kept, width)
    sums = jnp.zeros((slots, width), F32)
    for j0 in range(0, n_angle * kept, width):
        sel = jnp.where(voxel_col == lane + float(j0), 1.0, 0.0).astype(BF16)
        sums = sums + dot(sel, all_vals[j0 : j0 + width])
    picked[...] = sums.astype(BF16)
    for k0 in range(0, slots, FWD):
        rows = picked[pl.ds(k0, FWD), :]
        forward_step(k0, [rows * own for own in own_row])
    proj_parts[my_slab] = scatter_tiles(fwd[...] * live[...])
    proj_copies = slab_exchange(proj_parts, proj_send, proj_recv)

    block_id = lax.broadcasted_iota(jnp.int32, (kept, width), 0)

    def live_left(k, ids):
        row = jnp.broadcast_to(live[k : k + 1, :], (kept, width))
        left = jnp.where(ids == voxel_s[0, k], row, 0.0).astype(BF16)
        left_live[k] = left
        return left

    def residual_left(k, ids):
        row = jnp.broadcast_to(fwd[k : k + 1, :], (kept, width))
        return left_live[k] * row.astype(BF16)

    def backward(left_of, out_ref):
        totals = []
        shares = []
        for g in range(groups):
            share = lax.div(voxel_s[0, g * cap], kept)
            ids = block_id + share * kept
            total = jnp.zeros((kept, width), F32)
            for k0 in range(g * cap, (g + 1) * cap, 2 * BWD):
                left = [
                    jnp.concatenate([left_of(k + i, ids) for i in range(BWD)], axis=1)
                    for k in (k0, k0 + BWD)
                ]
                prod = dot(jnp.concatenate(left, axis=0), side_by_side(w, k0, BWD))
                total = total + (prod[:kept, :width] + prod[kept:, width:])
            totals.append(total)
            shares.append(jnp.full((kept, width), share, jnp.int32))
        for s in range(n_angle):
            out = jnp.where(shares[0] == s, totals[0], 0.0)
            for g in range(1, groups):
                out = jnp.where(shares[g] == s, totals[g], out)
            out_ref[s] = out

    backward(live_left, col_out)
    col_copies = angle_exchange(col_out, col_in, col_send, col_recv)

    meas_copy.wait()
    for c in row_copies:
        c.wait()
    row_sum = row_parts[0]
    for s in range(1, n_slab):
        row_sum = row_sum + row_parts[s]
    row_sum = jnp.maximum(row_sum, 1.0)
    for c in proj_copies:
        c.wait()
    proj = proj_parts[0]
    for s in range(1, n_slab):
        proj = proj + proj_parts[s]
    weighted = (meas[...] - proj) / row_sum
    res_buf[...] = weighted
    res_copy = pltpu.make_async_copy(res_buf, res_hbm, out_sem.at[0])
    res_copy.start()
    sel = jnp.where(tile_col == lane, 1.0, 0.0)[:, :tiles].astype(BF16)
    fwd[...] = dot(sel, weighted.astype(BF16))
    backward(residual_left, back_out)
    back_copies = angle_exchange(back_out, back_in, back_send, back_recv)

    back_in[my_angle] = back_out[my_angle]
    col_in[my_angle] = col_out[my_angle]
    for c in col_copies:
        c.wait()
    col_sum = col_in[0]
    for s in range(1, n_angle):
        col_sum = col_sum + col_in[s]
    col_sum = jnp.maximum(col_sum, 1.0)
    for c in back_copies:
        c.wait_recv()
    back = back_in[0]
    for s in range(1, n_angle):
        back = back + back_in[s]
    new_buf[...] = back / col_sum
    new_copy = pltpu.make_async_copy(new_buf, new_hbm, out_sem.at[1])
    new_copy.start()
    for c in vals_copies:
        c.wait_send()
    for c in back_copies:
        c.wait_send()
    res_copy.wait()
    new_copy.wait()


def on_device(volume, measured, footprint, block_voxel, block_tile, block_rows):
    n_slab = lax.axis_size("slab")
    n_angle = lax.axis_size("angle")
    kept, width = volume.shape
    tiles = measured.shape[0]
    slots = footprint.shape[0]
    cap = 2 * slots // n_angle
    any_space = pl.BlockSpec(memory_space=pl.ANY)
    dma = pltpu.SemaphoreType.DMA
    index = pltpu.VMEM((1, slots), jnp.int32)
    per_share = pltpu.VMEM((n_angle, kept, width), F32)
    per_slab = pltpu.VMEM((n_slab, tiles, width), F32)
    by_slot = pltpu.VMEM((slots, width), F32)
    new, res = pl.pallas_call(
        functools.partial(kernel, n_slab, n_angle, cap),
        out_shape=(
            jax.ShapeDtypeStruct(volume.shape, F32),
            jax.ShapeDtypeStruct(measured.shape, F32),
        ),
        in_specs=[any_space] * 6,
        out_specs=(any_space, any_space),
        scratch_shapes=[
            pltpu.VMEM(footprint.shape, BF16),
            pltpu.VMEM(footprint.shape, BF16),
            pltpu.VMEM(volume.shape, F32),
            pltpu.VMEM(measured.shape, F32),
            index, index, index,
            pltpu.SMEM((1, slots), jnp.int32),
            pltpu.VMEM((n_angle, kept, width), BF16),
            pltpu.VMEM((slots, width), BF16),
            by_slot, by_slot,
            pltpu.VMEM((tiles, slots), BF16),
            per_slab, per_slab,
            per_share, per_share, per_share, per_share,
            pltpu.VMEM(measured.shape, F32),
            pltpu.VMEM(volume.shape, F32),
            pltpu.VMEM((slots, kept, width), BF16),
            dma((PIECES,)), dma((6,)), dma((2,)),
            dma((n_angle - 1,)), dma((n_angle - 1,)),
            dma((n_slab - 1,)), dma((n_slab - 1,)),
            dma((n_slab - 1,)), dma((n_slab - 1,)),
            dma((n_angle - 1,)), dma((n_angle - 1,)),
            dma((n_angle - 1,)), dma((n_angle - 1,)),
        ],
        compiler_params=pltpu.CompilerParams(
            collective_id=0, has_side_effects=True, vmem_limit_bytes=56 * 1024 * 1024
        ),
        cost_estimate=pl.CostEstimate(
            flops=8 * slots * width * width, bytes_accessed=2 * slots * width * width, transcendentals=0
        ),
    )(
        volume, measured, footprint,
        block_voxel.reshape(1, slots), block_tile.reshape(1, slots), block_rows.reshape(1, slots),
    )
    return volume + new, res


def solution(mesh):
    in_specs = (
        P(("slab", "angle"), None),
        P("angle", None),
        P(("slab", "angle"), None, None),
        P(("slab", "angle")),
        P(("slab", "angle")),
        P(("slab", "angle")),
    )
    out_specs = (P(("slab", "angle"), None), P("angle", None))
    return jax.shard_map(
        on_device, mesh=mesh, in_specs=in_specs, out_specs=out_specs, check_vma=False
    )
```

```python
import functools

import jax
import jax.numpy as jnp
from jax import lax
from jax.experimental import pallas as pl
from jax.experimental.pallas import tpu as pltpu
from jax.sharding import PartitionSpec as P

MESH = pl.DeviceIdType.MESH
F32 = jnp.float32
BF16 = jnp.bfloat16
FWD = 16
BWD = 12
PIECES = 4


def dot(a, b):
    return jnp.dot(a, b, preferred_element_type=F32)


def three_terms(x):
    hi = x.astype(BF16)
    rest = x - hi.astype(F32)
    mid = rest.astype(BF16)
    lo = (rest - mid.astype(F32)).astype(BF16)
    return hi, mid, lo


def kernel(
    n_slab, n_angle, cap,
    vol_hbm, meas_hbm, foot_hbm, voxel_hbm, tile_hbm, rows_hbm,
    new_hbm, res_hbm,
    w, w_turned, vol, meas, voxel_v, tile_v, rows_v, voxel_s,
    slab_vals, picked, live, fwd, onehot_t, row_parts, proj_parts,
    col_out, col_in, back_out, back_in, res_buf, new_buf, left_live,
    piece_sem, local_sem, out_sem,
    vals_send, vals_recv, row_send, row_recv, proj_send, proj_recv,
    col_send, col_recv, back_send, back_recv,
):
    slots, width, _ = w.shape
    kept = vol.shape[0]
    tiles = meas.shape[0]
    groups = slots // cap
    piece = slots // PIECES
    my_slab = lax.axis_index("slab")
    my_angle = lax.axis_index("angle")

    def angle_peer(d):
        return lax.rem(my_angle + d, n_angle)

    def slab_peer(d):
        return lax.rem(my_slab + d, n_slab)

    vol_copy = pltpu.make_async_copy(vol_hbm, vol, local_sem.at[0])
    vol_copy.start()
    barrier = pltpu.get_barrier_semaphore()
    for d in range(1, n_angle):
        pl.semaphore_signal(barrier, inc=1, device_id={"angle": angle_peer(d)}, device_id_type=MESH)
    for d in range(1, n_slab):
        pl.semaphore_signal(barrier, inc=1, device_id={"slab": slab_peer(d)}, device_id_type=MESH)
    index_copies = [
        pltpu.make_async_copy(voxel_hbm, voxel_v, local_sem.at[1]),
        pltpu.make_async_copy(tile_hbm, tile_v, local_sem.at[2]),
        pltpu.make_async_copy(rows_hbm, rows_v, local_sem.at[3]),
        pltpu.make_async_copy(voxel_hbm, voxel_s, local_sem.at[4]),
    ]
    for c in index_copies:
        c.start()
    piece_copies = []
    for i in range(PIECES):
        span = pl.ds(i * piece, piece)
        c = pltpu.make_async_copy(foot_hbm.at[span], w.at[span], piece_sem.at[i])
        c.start()
        piece_copies.append(c)
    meas_copy = pltpu.make_async_copy(meas_hbm, meas, local_sem.at[5])
    meas_copy.start()

    vol_copy.wait()
    slab_vals[my_angle] = vol[...].astype(BF16)
    pl.semaphore_wait(barrier, n_angle + n_slab - 2)

    vals_copies = []
    for d in range(1, n_angle):
        c = pltpu.make_async_remote_copy(
            src_ref=slab_vals.at[my_angle], dst_ref=slab_vals.at[my_angle],
            send_sem=vals_send.at[d - 1], recv_sem=vals_recv.at[d - 1],
            device_id={"angle": angle_peer(d)}, device_id_type=MESH,
        )
        c.start()
        vals_copies.append(c)

    def slab_exchange(buf, send, recv):
        copies = []
        for d in range(1, n_slab):
            c = pltpu.make_async_remote_copy(
                src_ref=buf.at[my_slab], dst_ref=buf.at[my_slab],
                send_sem=send.at[d - 1], recv_sem=recv.at[d - 1],
                device_id={"slab": slab_peer(d)}, device_id_type=MESH,
            )
            c.start()
            copies.append(c)
        return copies

    def angle_exchange(out, into, send, recv):
        copies = []
        for d in range(1, n_angle):
            c = pltpu.make_async_remote_copy(
                src_ref=out.at[angle_peer(d)], dst_ref=into.at[my_angle],
                send_sem=send.at[d - 1], recv_sem=recv.at[d - 1],
                device_id={"angle": angle_peer(d)}, device_id_type=MESH,
            )
            c.start()
            copies.append(c)
        return copies

    for c in index_copies:
        c.wait()

    def down(ref):
        return jnp.broadcast_to(ref[...].astype(F32), (width, slots)).T

    voxel_col = down(voxel_v)
    tile_col = down(tile_v)
    lane = lax.broadcasted_iota(jnp.int32, (slots, width), 1).astype(F32)
    live[...] = jnp.where(lane < down(rows_v), 1.0, 0.0)
    tile_rows = lax.broadcasted_iota(jnp.int32, (tiles, slots), 0)
    onehot_t[...] = jnp.where(tile_rows == tile_v[...], 1.0, 0.0).astype(BF16)

    def scatter_tiles(values):
        terms = jnp.concatenate(three_terms(values), axis=1)
        out = dot(onehot_t[...], terms)
        return (out[:, 2 * width :] + out[:, width : 2 * width]) + out[:, :width]

    row_id = lax.broadcasted_iota(jnp.int32, (FWD, width), 0)
    own_row = [jnp.where(row_id == i, 1.0, 0.0).astype(BF16) for i in range(FWD)]

    def forward_step(k0, left):
        mats = w_turned[pl.ds(k0, FWD)].reshape(FWD * width, width)
        fwd[pl.ds(k0, FWD), :] = dot(jnp.concatenate(left, axis=1), mats)

    for i in range(PIECES):
        piece_copies[i].wait()
        for k0 in range(i * piece, (i + 1) * piece, FWD):
            for k in range(k0, k0 + FWD):
                w_turned[k] = w[k].T
            forward_step(k0, own_row)
    row_parts[my_slab] = scatter_tiles(fwd[...] * live[...])
    row_copies = slab_exchange(row_parts, row_send, row_recv)

    for c in vals_copies:
        c.wait_recv()
    all_vals = slab_vals[...].reshape(n_angle * kept, width)
    sums = jnp.zeros((slots, width), F32)
    for j0 in range(0, n_angle * kept, width):
        sel = jnp.where(voxel_col == lane + float(j0), 1.0, 0.0).astype(BF16)
        sums = sums + dot(sel, all_vals[j0 : j0 + width])
    picked[...] = sums.astype(BF16)
    for k0 in range(0, slots, FWD):
        rows = picked[pl.ds(k0, FWD), :]
        forward_step(k0, [rows * own for own in own_row])
    proj_parts[my_slab] = scatter_tiles(fwd[...] * live[...])
    proj_copies = slab_exchange(proj_parts, proj_send, proj_recv)

    block_id = lax.broadcasted_iota(jnp.int32, (kept, width), 0)

    def live_left(k, ids):
        row = jnp.broadcast_to(live[k : k + 1, :], (kept, width))
        left = jnp.where(ids == voxel_s[0, k], row, 0.0).astype(BF16)
        left_live[k] = left
        return left

    def live_sums(out_ref):
        totals = []
        shares = []
        for g in range(groups):
            share = lax.div(voxel_s[0, g * cap], kept)
            ids = block_id + share * kept
            total = jnp.zeros((kept, width), F32)
            for k0 in range(g * cap, (g + 1) * cap, BWD):
                cols = [live_left(k, ids) for k in range(k0, k0 + BWD)]
                mats = w[pl.ds(k0, BWD)].reshape(BWD * width, width)
                total = total + dot(jnp.concatenate(cols, axis=1), mats)
            totals.append(total)
            shares.append(jnp.full((kept, width), share, jnp.int32))
        for s in range(n_angle):
            out = jnp.where(shares[0] == s, totals[0], 0.0)
            for g in range(1, groups):
                out = jnp.where(shares[g] == s, totals[g], out)
            out_ref[s] = out

    live_sums(col_out)
    col_copies = angle_exchange(col_out, col_in, col_send, col_recv)

    meas_copy.wait()
    for c in row_copies:
        c.wait()
    row_sum = row_parts[0]
    for s in range(1, n_slab):
        row_sum = row_sum + row_parts[s]
    row_sum = jnp.maximum(row_sum, 1.0)
    for c in proj_copies:
        c.wait()
    proj = proj_parts[0]
    for s in range(1, n_slab):
        proj = proj + proj_parts[s]
    weighted = (meas[...] - proj) / row_sum
    res_buf[...] = weighted
    res_copy = pltpu.make_async_copy(res_buf, res_hbm, out_sem.at[0])
    res_copy.start()
    sel = jnp.where(tile_col == lane, 1.0, 0.0)[:, :tiles].astype(BF16)
    fwd[...] = dot(sel, weighted.astype(BF16))
    group_shares = [lax.div(voxel_s[0, g * cap], kept) for g in range(groups)]

    def residual_sums(share):
        first = jnp.int32(0)
        named = jnp.float32(0.0)
        for g in range(groups):
            here = group_shares[g] == share
            first = jnp.where(here, g * cap, first)
            named = jnp.where(here, 1.0, named)
        total = jnp.zeros((kept, width), F32)
        for k0 in range(0, cap, BWD):
            cols = []
            for k in range(k0, k0 + BWD):
                row = jnp.broadcast_to(fwd[pl.ds(first + k, 1), :], (kept, width))
                cols.append(left_live[first + k] * row.astype(BF16))
            mats = w[pl.ds(first + k0, BWD)].reshape(BWD * width, width)
            total = total + dot(jnp.concatenate(cols, axis=1), mats)
        return total * named

    back_copies = []
    for d in range(1, n_angle):
        back_out[d] = residual_sums(angle_peer(d))
        c = pltpu.make_async_remote_copy(
            src_ref=back_out.at[d], dst_ref=back_in.at[my_angle],
            send_sem=back_send.at[d - 1], recv_sem=back_recv.at[d - 1],
            device_id={"angle": angle_peer(d)}, device_id_type=MESH,
        )
        c.start()
        back_copies.append(c)
    back_in[my_angle] = residual_sums(my_angle)

    col_in[my_angle] = col_out[my_angle]
    for c in col_copies:
        c.wait()
    col_sum = col_in[0]
    for s in range(1, n_angle):
        col_sum = col_sum + col_in[s]
    col_sum = jnp.maximum(col_sum, 1.0)
    for c in back_copies:
        c.wait_recv()
    back = back_in[0]
    for s in range(1, n_angle):
        back = back + back_in[s]
    new_buf[...] = back / col_sum
    new_copy = pltpu.make_async_copy(new_buf, new_hbm, out_sem.at[1])
    new_copy.start()
    for c in vals_copies:
        c.wait_send()
    for c in back_copies:
        c.wait_send()
    res_copy.wait()
    new_copy.wait()


def on_device(volume, measured, footprint, block_voxel, block_tile, block_rows):
    n_slab = lax.axis_size("slab")
    n_angle = lax.axis_size("angle")
    kept, width = volume.shape
    tiles = measured.shape[0]
    slots = footprint.shape[0]
    cap = 2 * slots // n_angle
    any_space = pl.BlockSpec(memory_space=pl.ANY)
    dma = pltpu.SemaphoreType.DMA
    index = pltpu.VMEM((1, slots), jnp.int32)
    per_share = pltpu.VMEM((n_angle, kept, width), F32)
    per_slab = pltpu.VMEM((n_slab, tiles, width), F32)
    by_slot = pltpu.VMEM((slots, width), F32)
    new, res = pl.pallas_call(
        functools.partial(kernel, n_slab, n_angle, cap),
        out_shape=(
            jax.ShapeDtypeStruct(volume.shape, F32),
            jax.ShapeDtypeStruct(measured.shape, F32),
        ),
        in_specs=[any_space] * 6,
        out_specs=(any_space, any_space),
        scratch_shapes=[
            pltpu.VMEM(footprint.shape, BF16),
            pltpu.VMEM(footprint.shape, BF16),
            pltpu.VMEM(volume.shape, F32),
            pltpu.VMEM(measured.shape, F32),
            index, index, index,
            pltpu.SMEM((1, slots), jnp.int32),
            pltpu.VMEM((n_angle, kept, width), BF16),
            pltpu.VMEM((slots, width), BF16),
            by_slot, by_slot,
            pltpu.VMEM((tiles, slots), BF16),
            per_slab, per_slab,
            per_share, per_share, per_share, per_share,
            pltpu.VMEM(measured.shape, F32),
            pltpu.VMEM(volume.shape, F32),
            pltpu.VMEM((slots, kept, width), BF16),
            dma((PIECES,)), dma((6,)), dma((2,)),
            dma((n_angle - 1,)), dma((n_angle - 1,)),
            dma((n_slab - 1,)), dma((n_slab - 1,)),
            dma((n_slab - 1,)), dma((n_slab - 1,)),
            dma((n_angle - 1,)), dma((n_angle - 1,)),
            dma((n_angle - 1,)), dma((n_angle - 1,)),
        ],
        compiler_params=pltpu.CompilerParams(
            collective_id=0, has_side_effects=True, vmem_limit_bytes=56 * 1024 * 1024
        ),
        cost_estimate=pl.CostEstimate(
            flops=8 * slots * width * width, bytes_accessed=2 * slots * width * width, transcendentals=0
        ),
    )(
        volume, measured, footprint,
        block_voxel.reshape(1, slots), block_tile.reshape(1, slots), block_rows.reshape(1, slots),
    )
    return volume + new, res


def solution(mesh):
    in_specs = (
        P(("slab", "angle"), None),
        P("angle", None),
        P(("slab", "angle"), None, None),
        P(("slab", "angle")),
        P(("slab", "angle")),
        P(("slab", "angle")),
    )
    out_specs = (P(("slab", "angle"), None), P("angle", None))
    return jax.shard_map(
        on_device, mesh=mesh, in_specs=in_specs, out_specs=out_specs, check_vma=False
    )
```
